32 devices in a mesh: row: 4 (over y, x), col: 8 (over z, core).
Axes of the slice: x: 2, y: 2, z: 4, core: 2. Of those that a mesh axis runs over, the one named last changes fastest.
Arguments:
- features: bfloat16 [8192, 256], P(('col', 'row')), may hold values from -6 to 6
- cotangent: bfloat16 [8192, 256], P(('row', 'col')), may hold values from -1.5 to 1.5
- degrees: int32 [8192], P(('row', 'col')), may hold values from 8 to 40
- weight: bfloat16 [256, 256], replicated, may hold values from -0.375 to 0.375
- tile_rows: int32 [4, 8, 256], P('row', 'col'), may hold values from 0 to 15
- tile_cols: int32 [4, 8, 256], P('row', 'col'), may hold values from 0 to 7
- tile_bits: int32 [4, 8, 256, 16, 128], P('row', 'col'), may hold values from 0 to 255, as said below
- tile_count: int32 [4, 8], P('row', 'col'), may hold values from 16 to 256, as said below
Outputs:
- output: bfloat16 [8192, 256], P(('row', 'col'))
- weight_grad: float32 [256, 256], replicated
- input_grad: bfloat16 [8192, 256], P(('col', 'row'))
The draws below stay inside these ranges and needn't reach their ends.
Inputs may be any that keep to these rules, and one draw needn't show every extreme that they name: `tile_bits`: each word holds 8 entries of 0 or 1 in its low bits; tiles at the same position may repeat and then add. `tile_count`: some device has all 256 slots live and some device 256 // 16.
All inputs are finite; a program needn't handle non-finite values.
Results may differ from the reference program's by a relative error of at most 0.024.
Values may be sent and summed in bfloat16 or wider, within the bound.
A program may use at most 64 MiB of HBM per device.

```python
import math
import jax
import jax.numpy as jnp
from jax import lax

F = 256
TILE = 128
NP = 256
TILES_DEV = 256
NODES = 8192
TROWS = 16
TCOLS = 8
N_ROW = 4
N_COL = 8


def draw_tile_bits(key, part):
    shape = (N_ROW, N_COL, TILES_DEV, TILE // 8, TILE)
    packed = jnp.zeros(shape, jnp.int32)
    for bit_number in range(8):
        flags = (jax.random.randint(jax.random.fold_in(key, 101 + bit_number), shape, 0, TILE) == 0).astype(jnp.int32)
        packed = packed + flags * 2 ** bit_number
    return packed


def draw_tile_count(key, part):
    devices_all = N_ROW * N_COL
    counted = jax.random.randint(jax.random.fold_in(key, 7), (devices_all,), TILES_DEV // 16, TILES_DEV + 1)
    shuffled = jax.random.permutation(jax.random.fold_in(key, 8), devices_all)
    counted = counted.at[shuffled[0]].set(TILES_DEV)
    counted = counted.at[shuffled[1]].set(TILES_DEV // 16)
    return counted.astype(jnp.int32).reshape(N_ROW, N_COL)


def place_ends(drawn, stream_key, low, top_value):
    spot = [jax.random.randint(jax.random.fold_in(stream_key, axis), (), 0, length) for axis, length in enumerate(drawn.shape)]
    main_axis = drawn.shape.index(max(drawn.shape))
    next_to = spot[:main_axis] + [(spot[main_axis] + 1) % drawn.shape[main_axis]] + spot[main_axis + 1:]
    return drawn.at[tuple(spot)].set(low).at[tuple(next_to)].set(top_value)


def levels(key, dims, cuts, low, top_value):
    level = 1.0
    for dim, parts in cuts:
        draws = jax.random.uniform(jax.random.fold_in(jax.random.fold_in(key, 6), dim), (parts,), jnp.float32, low / len(cuts), top_value / len(cuts))
        level = level * jnp.repeat(jnp.exp(draws), dims[dim] // parts).reshape((-1,) + (1,) * (len(dims) - 1 - dim))
    return level


def centred(rng, dims, spread, limit, split=(), held_as=jnp.bfloat16):
    level = levels(rng, dims, split, -0.22, 0.18) if split else 1.0
    array = jax.random.normal(rng, dims, jnp.float32) * spread * level
    return jnp.minimum(jnp.maximum(array, -limit), limit).astype(held_as)


def setup_inputs(seed: int = 0) -> dict:
    splits = jax.random.split(jax.random.key(seed), 9)
    features = centred(splits[0], (NODES, F), 1.0, 6.0, ((0, 32),))
    cotangent = centred(splits[1], (NODES, F), 0.25, 1.5, ((0, 32),))
    degrees = place_ends(jax.random.randint(splits[2], (NODES,), 8, 41), jax.random.fold_in(splits[2], 1), 8, 40).astype(jnp.int32)
    weight = centred(splits[3], (F, F), F ** -0.5, 0.375)
    tile_rows = place_ends(jax.random.randint(splits[4], (N_ROW, N_COL, TILES_DEV), 0, TROWS), jax.random.fold_in(splits[4], 1), 0, TROWS - 1).astype(jnp.int32)
    tile_cols = place_ends(jax.random.randint(splits[5], (N_ROW, N_COL, TILES_DEV), 0, TCOLS), jax.random.fold_in(splits[5], 1), 0, TCOLS - 1).astype(jnp.int32)
    tile_bits = draw_tile_bits(jax.random.fold_in(splits[8], 71), 0)
    tile_count = draw_tile_count(jax.random.fold_in(splits[8], 71), 0)
    return dict(features=features, cotangent=cotangent, degrees=degrees, weight=weight, tile_rows=tile_rows, tile_cols=tile_cols, tile_bits=tile_bits, tile_count=tile_count)


def unpack(packed):
    shifts = jnp.arange(8, dtype=jnp.int32)
    flags = jnp.right_shift(packed[:, :, None, :], shifts[None, None, :, None]) & 1
    return flags.reshape(packed.shape[0], packed.shape[1] * 8, packed.shape[2])


def sweep_tiles(packed, row_ids, col_ids, live_count, source, out_tiles, forward):
    block_size = math.gcd(TILES_DEV, 32)

    def one_block(totals, position):
        offset = position * block_size
        block_bits = lax.dynamic_slice_in_dim(packed, offset, block_size, 0)
        block_rows = lax.dynamic_slice_in_dim(row_ids, offset, block_size, 0)
        block_cols = lax.dynamic_slice_in_dim(col_ids, offset, block_size, 0)
        live_mask = (offset + jnp.arange(block_size, dtype=jnp.int32)) < live_count
        pattern = (unpack(block_bits) * live_mask.astype(jnp.int32)[:, None, None]).astype(jnp.float32)
        if forward:
            product = jnp.einsum("bji,bjf->bif", pattern, source[block_cols])
            return totals.at[block_rows].add(product), None
        product = jnp.einsum("bji,bif->bjf", pattern, source[block_rows])
        return totals.at[block_cols].add(product), None

    initial = jnp.zeros((out_tiles, TILE, F), jnp.float32)
    totals, _ = lax.scan(one_block, initial, jnp.arange(TILES_DEV // block_size, dtype=jnp.int32))
    return totals


def rounded(values):
    return lax.optimization_barrier(values.astype(jnp.bfloat16)).astype(jnp.float32)


def reference(features, cotangent, degrees, weight, tile_rows, tile_cols, tile_bits, tile_count):
    rows_block = NP * N_COL
    cols_block = NP * N_ROW
    degree_values = degrees.astype(jnp.float32)
    feature_tiles = features.astype(jnp.float32).reshape(N_COL, cols_block // TILE, TILE, F)
    scaled = (cotangent.astype(jnp.float32) / degree_values[:, None]).astype(jnp.bfloat16)
    gradient_tiles = scaled.astype(jnp.float32).reshape(N_ROW, rows_block // TILE, TILE, F)

    def forward_row(row_block):
        def add_column(running, col_block):
            partial_value = sweep_tiles(tile_bits[row_block, col_block], tile_rows[row_block, col_block],
                                  tile_cols[row_block, col_block], tile_count[row_block, col_block],
                                  feature_tiles[col_block], rows_block // TILE, True)
            return running + rounded(partial_value), None
        start_sum = jnp.zeros((rows_block // TILE, TILE, F), jnp.float32)
        running, _ = lax.scan(add_column, start_sum, jnp.arange(N_COL, dtype=jnp.int32))
        return running.reshape(rows_block, F)

    def backward_column(col_block):
        def add_row(running, row_block):
            partial_value = sweep_tiles(tile_bits[row_block, col_block], tile_rows[row_block, col_block],
                                  tile_cols[row_block, col_block], tile_count[row_block, col_block],
                                  gradient_tiles[row_block], cols_block // TILE, False)
            return running + rounded(partial_value), None
        start_sum = jnp.zeros((cols_block // TILE, TILE, F), jnp.float32)
        running, _ = lax.scan(add_row, start_sum, jnp.arange(N_ROW, dtype=jnp.int32))
        return running.reshape(cols_block, F)

    summed = lax.map(forward_row, jnp.arange(N_ROW, dtype=jnp.int32)).reshape(NODES, F)
    aggregated = (summed / degree_values[:, None]).astype(jnp.bfloat16)
    output = jnp.dot(aggregated, weight, preferred_element_type=jnp.float32).astype(jnp.bfloat16)
    weight_grad = jnp.dot(aggregated.T, cotangent, preferred_element_type=jnp.float32)
    propagated = lax.map(backward_column, jnp.arange(N_COL, dtype=jnp.int32)).reshape(NODES, F)
    input_grad = jnp.dot(propagated.astype(jnp.bfloat16), weight.T, preferred_element_type=jnp.float32).astype(jnp.bfloat16)
    return output, weight_grad, input_grad
```

```python
import functools

import jax
import jax.numpy as jnp
from jax import lax
from jax.experimental import pallas as pl
from jax.experimental.pallas import tpu as pltpu
from jax.sharding import PartitionSpec as P

SMEM = pltpu.SMEM
VMEM = pltpu.VMEM
BF16 = jnp.bfloat16
F32 = jnp.float32


def build_kernel(trows, chunk, count_ref, rows_ref, cols_ref, bits_ref, out_ref, acc0, acc1):
    base = pl.program_id(0) * chunk
    zero = jnp.zeros(acc0.shape[1:], jnp.int32)

    def clear(p, carry):
        acc0[p] = zero
        acc1[p] = zero
        return carry

    lax.fori_loop(0, chunk * trows, clear, 0, unroll=4)
    count = count_ref[0]

    def add_pair(k, carry):
        for half, acc in enumerate((acc0, acc1)):
            s = 2 * k + half
            col = cols_ref[s] - base
            ok = (s < count) & (col >= 0) & (col < chunk)
            p = jnp.where(ok, col * trows + rows_ref[s], 0)
            words = bits_ref[s]
            word = (words[:8] | (words[8:] << 16)) & (0 - ok.astype(jnp.int32))
            for b in range(8):
                acc[p, b] += (word >> b) & 0x10001
        return carry

    lax.fori_loop(0, (count + 1) // 2, add_pair, 0)

    def convert(row, carry):
        lanes = pl.ds(pl.multiple_of(row * 128, 128), 128)
        for col in range(chunk):
            p = col * trows + row
            for b in range(8):
                v = acc0[p, b] + acc1[p, b]
                both = jnp.concatenate([v & 0xFFFF, v >> 16], axis=0)
                out_ref[pl.ds(col * 128 + b * 16, 16), lanes] = both.astype(F32).astype(BF16)
        return carry

    lax.fori_loop(0, trows, convert, 0)


def build_adjacency(count, rows, cols, bits, trows, tcols):
    chunk = max(d for d in range(1, tcols + 1) if tcols % d == 0 and d * trows <= 128)
    scratch = pltpu.VMEM((chunk * trows, 8, 8, 128), jnp.int32)
    return pl.pallas_call(
        functools.partial(build_kernel, trows, chunk),
        grid=(tcols // chunk,),
        out_shape=jax.ShapeDtypeStruct((tcols * 128, trows * 128), BF16),
        in_specs=[
            pl.BlockSpec(memory_space=SMEM),
            pl.BlockSpec(memory_space=SMEM),
            pl.BlockSpec(memory_space=SMEM),
            pl.BlockSpec(memory_space=VMEM),
        ],
        out_specs=pl.BlockSpec((chunk * 128, trows * 128), lambda g: (g, 0)),
        scratch_shapes=[scratch, scratch],
        compiler_params=pltpu.CompilerParams(vmem_limit_bytes=40 * 2**20),
        name="build_adjacency",
    )(count, rows, cols, bits)


def swap_order(x, a, b):
    return x.reshape(-1, a, b, x.shape[-1]).swapaxes(1, 2).reshape(x.shape)


def per_device(features, cotangent, degrees, weight, tile_rows, tile_cols, tile_bits, tile_count):
    nodes, width = features.shape
    trows = nodes * lax.axis_size("col") // 128
    tcols = nodes * lax.axis_size("row") // 128
    at = build_adjacency(
        tile_count[0], tile_rows[0, 0], tile_cols[0, 0], tile_bits[0, 0], trows, tcols
    )
    deg = degrees[:, None].astype(F32)
    scaled = (cotangent.astype(F32) / deg).astype(BF16)
    feats = lax.all_gather(swap_order(features, 16, 8), "row", axis=0, tiled=True)
    grads = lax.all_gather(scaled, "col", axis=0, tiled=True)
    fwd = lax.dot_general(at, feats, (((0,), (0,)), ((), ())), preferred_element_type=F32)
    fwd = fwd.astype(BF16)
    local = lax.dot_general(fwd, grads, (((0,), (0,)), ((), ())), preferred_element_type=F32)
    weight_grad = lax.psum(local, ("row", "col"))
    summed = lax.psum_scatter(fwd, "col", scatter_dimension=0, tiled=True).astype(F32)
    aggregated = (summed / deg).astype(BF16)
    output = jnp.dot(aggregated, weight, preferred_element_type=F32).astype(BF16)
    bwd = jnp.dot(at, grads, preferred_element_type=F32).astype(BF16)
    back = swap_order(lax.psum_scatter(bwd, "row", scatter_dimension=0, tiled=True), 8, 16)
    input_grad = jnp.dot(back, weight.T, preferred_element_type=F32).astype(BF16)
    return output, weight_grad, input_grad


def solution(mesh):
    placed = (
        P(("col", "row"), None),
        P(("row", "col"), None),
        P(("row", "col")),
        P(),
        P("row", "col", None),
        P("row", "col", None),
        P("row", "col", None, None, None),
        P("row", "col"),
    )
    return jax.shard_map(
        per_device,
        mesh=mesh,
        in_specs=placed,
        out_specs=(P(("row", "col"), None), P(), P(("col", "row"), None)),
        check_vma=False,
    )
```

```python
import functools

import jax
import jax.numpy as jnp
from jax import lax
from jax.experimental import pallas as pl
from jax.experimental.pallas import tpu as pltpu
from jax.sharding import PartitionSpec as P

SMEM = pltpu.SMEM
VMEM = pltpu.VMEM
BF16 = jnp.bfloat16
F32 = jnp.float32


def build_kernel(trows, chunk, count_ref, rows_ref, cols_ref, bits_ref, out_ref, acc0, acc1):
    base = pl.program_id(0) * chunk
    zero = jnp.zeros(acc0.shape[1:], jnp.int32)

    def clear(p, carry):
        acc0[p] = zero
        acc1[p] = zero
        return carry

    lax.fori_loop(0, chunk * trows, clear, 0, unroll=4)
    count = count_ref[0]

    def add_pair(k, carry):
        for half, acc in enumerate((acc0, acc1)):
            s = 2 * k + half
            col = cols_ref[s] - base
            ok = (s < count) & (col >= 0) & (col < chunk)
            p = jnp.where(ok, col * trows + rows_ref[s], 0)
            words = bits_ref[s]
            word = (words[:8] | (words[8:] << 16)) & (0 - ok.astype(jnp.int32))
            for b in range(8):
                acc[p, b] += (word >> b) & 0x10001
        return carry

    lax.fori_loop(0, (count + 1) // 2, add_pair, 0)

    def convert(row, carry):
        lanes = pl.ds(pl.multiple_of(row * 128, 128), 128)
        for col in range(chunk):
            p = col * trows + row
            for b in range(8):
                v = acc0[p, b] + acc1[p, b]
                both = jnp.concatenate([v & 0xFFFF, v >> 16], axis=0)
                out_ref[pl.ds(col * 128 + b * 16, 16), lanes] = both.astype(F32).astype(BF16)
        return carry

    lax.fori_loop(0, trows, convert, 0)


def build_adjacency(count, rows, cols, bits, trows, tcols):
    chunk = max(d for d in range(1, tcols + 1) if tcols % d == 0 and d * trows <= 128)
    scratch = pltpu.VMEM((chunk * trows, 8, 8, 128), jnp.int32)
    return pl.pallas_call(
        functools.partial(build_kernel, trows, chunk),
        grid=(tcols // chunk,),
        out_shape=jax.ShapeDtypeStruct((tcols * 128, trows * 128), BF16),
        in_specs=[
            pl.BlockSpec(memory_space=SMEM),
            pl.BlockSpec(memory_space=SMEM),
            pl.BlockSpec(memory_space=SMEM),
            pl.BlockSpec(memory_space=VMEM),
        ],
        out_specs=pl.BlockSpec((chunk * 128, trows * 128), lambda g: (g, 0)),
        scratch_shapes=[scratch, scratch],
        compiler_params=pltpu.CompilerParams(vmem_limit_bytes=40 * 2**20),
        name="build_adjacency",
    )(count, rows, cols, bits)


MESH = pl.DeviceIdType.MESH


def copy_to(src, dst, send_sem, recv_sem, device):
    return pltpu.make_async_remote_copy(
        src_ref=src,
        dst_ref=dst,
        send_sem=send_sem,
        recv_sem=recv_sem,
        device_id=device,
        device_id_type=MESH,
    )


def dot(a, b, dims=((1,), (0,))):
    return lax.dot_general(a, b, (dims, ((), ())), preferred_element_type=F32)


def layer_kernel(
    n_row, n_z,
    at_ref, feat_ref, cot_ref, deg_ref, weight_ref,
    out_ref, wgrad_ref, igrad_ref,
    feats, grads, part, pair, sums, arrived, back, back_in, w_part, w_in, w_all,
    feat_s, feat_r, grad_s, grad_r, relay_s, pair_s, pair_r, sum_s, sum_r, back_s, back_r,
    w1_s, w1_r, w2_s, w2_r,
):
    n = feat_ref.shape[0]
    n_col = 2 * n_z
    n_all = n_row * n_col
    r = lax.axis_index("row")
    c = lax.axis_index("col")
    me = r * n_col + c
    z = c // 2
    core = c % 2
    sibling = (r, z * 2 + 1 - core)

    def peer_of(i):
        peer = (me + i) % n_all
        return peer, (peer // n_col, peer % n_col)

    barrier = pltpu.get_barrier_semaphore()

    @pl.loop(1, n_all)
    def _(i):
        pl.semaphore_signal(barrier, inc=1, device_id=peer_of(i)[1], device_id_type=MESH)

    i0 = lax.broadcasted_iota(jnp.int32, (n, n), 0)
    i1 = lax.broadcasted_iota(jnp.int32, (n, n), 1)
    placed = (i1 // 128) * 128 + (i1 % 16) * 8 + (i1 % 128) // 16
    order = (i0 == placed).astype(F32).astype(BF16)
    deg_row = deg_ref[...].astype(F32)
    deg_col = jnp.sum(jnp.where(i0 == i1, deg_row, 0.0), axis=1, keepdims=True)
    grads[c] = (cot_ref[...].astype(F32) / deg_col).astype(BF16)
    feats[r] = dot(feat_ref[...], order, ((0,), (0,))).astype(BF16)

    pl.semaphore_wait(barrier, n_all - 1)

    def feat_copy(i):
        q = (r + i) % n_row
        return q, copy_to(feats.at[r], feats.at[r], feat_s.at[q], feat_r.at[r], (q, c))

    def grad_copy(i):
        q = ((z + i) % n_z) * 2 + core
        return q, copy_to(grads.at[c], grads.at[c], grad_s.at[q], grad_r.at[c], (r, q))

    def relay_copy(q):
        return copy_to(grads.at[q], grads.at[q], relay_s.at[q // 2], grad_r.at[q], sibling)

    for i in range(1, n_row):
        feat_copy(i)[1].start()
    for i in range(1, n_z):
        grad_copy(i)[1].start()
    relay_copy(c).start()

    def arrive(ref, sem, slot):
        copy_to(ref.at[slot], ref.at[slot], sem.at[slot], sem.at[slot], sibling).wait_recv()

    for i in range(1, n_row):
        arrive(feats, feat_r, (r + i) % n_row)

    def forward(q):
        lanes = pl.ds(pl.multiple_of(q * n, n), n)
        total = dot(feats[0], at_ref[pl.ds(0, n), lanes])
        for k in range(1, n_row):
            total += dot(feats[k], at_ref[pl.ds(k * n, n), lanes])
        part[q] = total.astype(BF16)

    def pair_copy(zz):
        q = zz * 2 + 1 - core
        return copy_to(part.at[q], pair.at[zz], pair_s.at[zz], pair_r.at[zz], sibling)

    @pl.loop(1, n_z + 1)
    def _(i):
        zz = (z + i) % n_z
        forward(zz * 2 + 1 - core)
        pair_copy(zz).start()

    @pl.loop(1, n_z + 1)
    def _(i):
        forward(((z + i) % n_z) * 2 + core)

    def sum_copy(i):
        zz = (z + i) % n_z
        return copy_to(
            sums.at[zz], arrived.at[z], sum_s.at[zz], sum_r.at[z], (r, zz * 2 + core)
        )

    @pl.loop(1, n_z)
    def _(i):
        zz = (z + i) % n_z
        arrive(pair, pair_r, zz)
        sums[zz] = (part[zz * 2 + core].astype(F32) + pair[zz].astype(F32)).astype(BF16)
        sum_copy(i).start()

    for i in range(1, n_z):
        q = ((z + i) % n_z) * 2 + core
        arrive(grads, grad_r, q)
        relay_copy(q).start()
    for i in range(n_z):
        arrive(grads, grad_r, ((z + i) % n_z) * 2 + 1 - core)

    def back_copy(q):
        return copy_to(back.at[q], back_in.at[r], back_s.at[q], back_r.at[r], (q, c))

    def backward(q):
        rows = pl.ds(pl.multiple_of(q * n, n), n)
        back[q] = dot(at_ref[rows, :], grads[...].reshape(n_col * n, -1)).astype(BF16)

    @pl.loop(1, n_row)
    def _(i):
        q = (r + i) % n_row
        backward(q)
        back_copy(q).start()

    local = dot(part[0], grads[0])
    for q in range(1, n_col):
        local += dot(part[q], grads[q])
    blocks = [(pl.ds((d // 2) * 16, 16), pl.ds((d % 2) * 128, 128)) for d in range(n_all)]
    rounded = local.astype(BF16)
    for d in range(n_all):
        top, left = (d // 2) * 16, (d % 2) * 128
        w_part[d] = rounded[top : top + 16, left : left + 128]

    def w1_copy(i):
        peer, device = peer_of(i)
        return copy_to(w_part.at[peer], w_in.at[me], w1_s.at[peer], w1_r.at[me], device)

    def w2_copy(i):
        peer, device = peer_of(i)
        return copy_to(w_all.at[me], w_all.at[me], w2_s.at[peer], w2_r.at[me], device)

    @pl.loop(1, n_all)
    def _(i):
        w1_copy(i).start()

    backward(r)
    w_in[me] = w_part[me]

    @pl.loop(1, n_all)
    def _(i):
        arrive(w_in, w1_r, (me + i) % n_all)

    w_all[me] = jnp.sum(w_in[...].astype(F32), axis=0).astype(BF16)

    @pl.loop(1, n_all)
    def _(i):
        w2_copy(i).start()

    arrive(pair, pair_r, z)
    total = part[c].astype(F32) + pair[z].astype(F32)
    for i in range(1, n_z):
        zz = (z + i) % n_z
        arrive(arrived, sum_r, zz)
        total += arrived[zz].astype(F32)
    out_ref[...] = dot((total / deg_row).astype(BF16), weight_ref[...], ((0,), (0,))).astype(BF16)

    total = back[r].astype(F32)
    for i in range(1, n_row):
        q = (r + i) % n_row
        arrive(back_in, back_r, q)
        total += back_in[q].astype(F32)
    ordered = dot(order, total.astype(BF16)).astype(BF16)
    igrad_ref[...] = dot(ordered, weight_ref[...], ((1,), (1,))).astype(BF16)

    @pl.loop(1, n_all)
    def _(i):
        arrive(w_all, w2_r, (me + i) % n_all)

    for d in range(n_all):
        wgrad_ref[blocks[d]] = w_all[d].astype(F32)

    for i in range(1, n_row):
        feat_copy(i)[1].wait_send()
        back_copy((r + i) % n_row).wait_send()
    for i in range(1, n_z):
        grad_copy(i)[1].wait_send()
        sum_copy(i).wait_send()
    for i in range(n_z):
        zz = (z + i) % n_z
        relay_copy(zz * 2 + core).wait_send()
        pair_copy(zz).wait_send()

    @pl.loop(1, n_all)
    def _(i):
        w1_copy(i).wait_send()
        w2_copy(i).wait_send()


def layer(at, features, cotangent, degrees, weight, n_row, n_z):
    n, width = features.shape
    n_col = 2 * n_z
    n_all = n_row * n_col
    block = lambda k: pltpu.VMEM((k, n, width), BF16)
    sems = lambda k: pltpu.SemaphoreType.DMA((k,))
    small = pltpu.VMEM((n_all, 16, 128), BF16)
    tile = jax.ShapeDtypeStruct((n, width), BF16)
    return pl.pallas_call(
        functools.partial(layer_kernel, n_row, n_z),
        out_shape=(tile, jax.ShapeDtypeStruct((width, width), F32), tile),
        in_specs=[pl.BlockSpec(memory_space=VMEM)] * 5,
        out_specs=(pl.BlockSpec(memory_space=VMEM),) * 3,
        scratch_shapes=[
            block(n_row), block(n_col), block(n_col), block(n_z), block(n_z), block(n_z),
            block(n_row), block(n_row), small, small, small,
            sems(n_row), sems(n_row), sems(n_col), sems(n_col), sems(n_z), sems(n_z), sems(n_z),
            sems(n_z), sems(n_z), sems(n_row), sems(n_row),
            sems(n_all), sems(n_all), sems(n_all), sems(n_all),
        ],
        compiler_params=pltpu.CompilerParams(
            collective_id=0, has_side_effects=True, vmem_limit_bytes=48 * 2**20
        ),
        name="layer",
    )(at, features, cotangent, degrees, weight)


def swap_order(x, a, b):
    return x.reshape(-1, a, b, x.shape[-1]).swapaxes(1, 2).reshape(x.shape)


def per_device(features, cotangent, degrees, weight, tile_rows, tile_cols, tile_bits, tile_count):
    nodes, width = features.shape
    trows = nodes * lax.axis_size("col") // 128
    tcols = nodes * lax.axis_size("row") // 128
    at = build_adjacency(
        tile_count[0], tile_rows[0, 0], tile_cols[0, 0], tile_bits[0, 0], trows, tcols
    )
    n_row, n_col = lax.axis_size("row"), lax.axis_size("col")
    if n_row * n_col * 16 * 128 == width * width and nodes == width:
        return layer(
            at, features, cotangent, degrees.reshape(1, nodes), weight, n_row, n_col // 2
        )
    deg = degrees[:, None].astype(F32)
    scaled = (cotangent.astype(F32) / deg).astype(BF16)
    feats = lax.all_gather(swap_order(features, 16, 8), "row", axis=0, tiled=True)
    grads = lax.all_gather(scaled, "col", axis=0, tiled=True)
    fwd = lax.dot_general(at, feats, (((0,), (0,)), ((), ())), preferred_element_type=F32)
    fwd = fwd.astype(BF16)
    local = lax.dot_general(fwd, grads, (((0,), (0,)), ((), ())), preferred_element_type=F32)
    weight_grad = lax.psum(local, ("row", "col"))
    summed = lax.psum_scatter(fwd, "col", scatter_dimension=0, tiled=True).astype(F32)
    aggregated = (summed / deg).astype(BF16)
    output = jnp.dot(aggregated, weight, preferred_element_type=F32).astype(BF16)
    bwd = jnp.dot(at, grads, preferred_element_type=F32).astype(BF16)
    back = swap_order(lax.psum_scatter(bwd, "row", scatter_dimension=0, tiled=True), 8, 16)
    input_grad = jnp.dot(back, weight.T, preferred_element_type=F32).astype(BF16)
    return output, weight_grad, input_grad


def solution(mesh):
    placed = (
        P(("col", "row"), None),
        P(("row", "col"), None),
        P(("row", "col")),
        P(),
        P("row", "col", None),
        P("row", "col", None),
        P("row", "col", None, None, None),
        P("row", "col"),
    )
    return jax.shard_map(
        per_device,
        mesh=mesh,
        in_specs=placed,
        out_specs=(P(("row", "col"), None), P(), P(("col", "row"), None)),
        check_vma=False,
    )
```

```python
import functools

import jax
import jax.numpy as jnp
from jax import lax
from jax.experimental import pallas as pl
from jax.experimental.pallas import tpu as pltpu
from jax.sharding import PartitionSpec as P

SMEM = pltpu.SMEM
VMEM = pltpu.VMEM
BF16 = jnp.bfloat16
F32 = jnp.float32


def build_kernel(trows, chunk, count_ref, rows_ref, cols_ref, bits_ref, out_ref, acc0, acc1):
    base = pl.program_id(0) * chunk
    zero = jnp.zeros(acc0.shape[1:], jnp.int32)

    def clear(p, carry):
        acc0[p] = zero
        acc1[p] = zero
        return carry

    lax.fori_loop(0, chunk * trows, clear, 0, unroll=4)
    count = count_ref[0]

    def add_pair(k, carry):
        for half, acc in enumerate((acc0, acc1)):
            s = 2 * k + half
            col = cols_ref[s] - base
            ok = (s < count) & (col >= 0) & (col < chunk)
            p = jnp.where(ok, col * trows + rows_ref[s], 0)
            words = bits_ref[s]
            word = (words[:8] | (words[8:] << 16)) & (0 - ok.astype(jnp.int32))
            for b in range(8):
                acc[p, b] += (word >> b) & 0x10001
        return carry

    lax.fori_loop(0, (count + 1) // 2, add_pair, 0)

    def convert(row, carry):
        lanes = pl.ds(pl.multiple_of(row * 128, 128), 128)
        for col in range(chunk):
            p = col * trows + row
            for b in range(8):
                v = acc0[p, b] + acc1[p, b]
                both = jnp.concatenate([v & 0xFFFF, v >> 16], axis=0)
                out_ref[pl.ds(col * 128 + b * 16, 16), lanes] = both.astype(F32).astype(BF16)
        return carry

    lax.fori_loop(0, trows, convert, 0)


def build_adjacency(count, rows, cols, bits, trows, tcols):
    chunk = max(d for d in range(1, tcols + 1) if tcols % d == 0 and d * trows <= 128)
    scratch = pltpu.VMEM((chunk * trows, 8, 8, 128), jnp.int32)
    return pl.pallas_call(
        functools.partial(build_kernel, trows, chunk),
        grid=(tcols // chunk,),
        out_shape=jax.ShapeDtypeStruct((tcols * 128, trows * 128), BF16),
        in_specs=[
            pl.BlockSpec(memory_space=SMEM),
            pl.BlockSpec(memory_space=SMEM),
            pl.BlockSpec(memory_space=SMEM),
            pl.BlockSpec(memory_space=VMEM),
        ],
        out_specs=pl.BlockSpec((chunk * 128, trows * 128), lambda g: (g, 0)),
        scratch_shapes=[scratch, scratch],
        compiler_params=pltpu.CompilerParams(vmem_limit_bytes=40 * 2**20),
        name="build_adjacency",
    )(count, rows, cols, bits)


MESH = pl.DeviceIdType.MESH


def copy_to(src, dst, send_sem, recv_sem, device):
    return pltpu.make_async_remote_copy(
        src_ref=src,
        dst_ref=dst,
        send_sem=send_sem,
        recv_sem=recv_sem,
        device_id=device,
        device_id_type=MESH,
    )


def dot(a, b, dims=((1,), (0,))):
    return lax.dot_general(a, b, (dims, ((), ())), preferred_element_type=F32)


def layer_kernel(
    n_row, n_z,
    rows_ref, cols_ref, count_ref, deg_ref, bits_hbm, feat_hbm, cot_hbm, weight_hbm,
    out_ref, wgrad_ref, igrad_ref,
    at_ref, prefix, plan, plan_smem, bits_ref, feat_ref, cot_ref, weight_ref, load_s, plan_s,
    feats, grads, part, pair, sums, arrived, back, back_in, w_part, w_in, w_mid, w_all,
    feat_s, feat_r, grad_s, grad_r, relay_s, pair_s, pair_r, sum_s, sum_r, back_s, back_r,
    w1_s, w1_r, w2_s, w2_r, w3_s, w3_r,
):
    n = feat_ref.shape[0]
    n_col = 2 * n_z
    n_plane = n_row * 2
    r = lax.axis_index("row")
    c = lax.axis_index("col")
    z = c // 2
    core = c % 2
    sibling = (r, z * 2 + 1 - core)

    me = r * 2 + core

    def plane_peer(i):
        q = (me + i) % n_plane
        return q, (q // 2, z * 2 + q % 2)

    def z_peer(i):
        zz = (z + i) % n_z
        return zz, (r, zz * 2 + core)

    barrier = pltpu.get_barrier_semaphore()
    for i in range(1, n_plane):
        pl.semaphore_signal(barrier, inc=1, device_id=plane_peer(i)[1], device_id_type=MESH)
    for i in range(1, n_z):
        pl.semaphore_signal(barrier, inc=1, device_id=z_peer(i)[1], device_id_type=MESH)
    loads = [
        pltpu.make_async_copy(src, dst, load_s.at[k])
        for k, (src, dst) in enumerate(
            ((cot_hbm, cot_ref), (feat_hbm, feat_ref), (bits_hbm, bits_ref), (weight_hbm, weight_ref))
        )
    ]
    for load in loads:
        load.start()

    i0 = lax.broadcasted_iota(jnp.int32, (n, n), 0)
    i1 = lax.broadcasted_iota(jnp.int32, (n, n), 1)
    placed = (i1 // 128) * 128 + (i1 % 16) * 8 + (i1 % 128) // 16
    order = (i0 == placed).astype(F32).astype(BF16)
    deg_row = deg_ref[...].astype(F32)
    deg_col = jnp.sum(jnp.where(i0 == i1, deg_row, 0.0), axis=1, keepdims=True)

    trows = n * n_col // 128
    tcols = n * n_row // 128
    places = trows * tcols
    slots = rows_ref.shape[1]
    s0 = lax.broadcasted_iota(jnp.int32, (slots, slots), 0)
    s1 = lax.broadcasted_iota(jnp.int32, (slots, slots), 1)
    lane = lax.broadcasted_iota(jnp.int32, (1, slots), 1)
    place = jnp.where(lane < count_ref[...], cols_ref[...] * trows + rows_ref[...], places)
    key_row = (place * slots + lane).astype(F32)
    key_col = jnp.sum(jnp.where(s0 == s1, key_row, 0.0), axis=1, keepdims=True)
    rank = jnp.sum((key_row < key_col).astype(F32), axis=1, keepdims=True)
    picked = jnp.where(rank == s1.astype(F32), s0, 0)
    before = (key_col < (s1 * slots).astype(F32)).astype(jnp.int32)
    plan[0:1, :] = jnp.clip(jnp.sum(picked, axis=0, keepdims=True), 0, slots - 1)
    plan[1:2, :] = jnp.clip(jnp.sum(before, axis=0, keepdims=True), 0, slots)
    plan_copy = pltpu.make_async_copy(plan, plan_smem, plan_s)
    plan_copy.start()

    loads[0].wait()
    loads[1].wait()
    grads[c] = (cot_ref[...].astype(F32) / deg_col).astype(BF16)
    feats[r] = dot(feat_ref[...], order, ((0,), (0,))).astype(BF16)

    pl.semaphore_wait(barrier, n_plane + n_z - 2)

    def feat_copy(i):
        q = (r + i) % n_row
        return q, copy_to(feats.at[r], feats.at[r], feat_s.at[q], feat_r.at[r], (q, c))

    def grad_copy(i):
        q = ((z + i) % n_z) * 2 + core
        return q, copy_to(grads.at[c], grads.at[c], grad_s.at[q], grad_r.at[c], (r, q))

    def relay_copy(q):
        return copy_to(grads.at[q], grads.at[q], relay_s.at[q // 2], grad_r.at[q], sibling)

    for i in range(1, n_row):
        feat_copy(i)[1].start()
    for i in range(1, n_z):
        grad_copy(i)[1].start()
    relay_copy(c).start()

    def arrive(ref, sem, slot):
        copy_to(ref.at[slot], ref.at[slot], sem.at[slot], sem.at[slot], sibling).wait_recv()

    plan_copy.wait()
    loads[2].wait()
    zero = jnp.zeros((8, 128), jnp.int32)
    for b in range(8):
        prefix[0, b] = zero

    def add_slot(k, totals):
        words = bits_ref[plan_smem[0, k]]
        word = words[:8] | (words[8:] << 16)
        totals = tuple(t + ((word >> b) & 0x10001) for b, t in enumerate(totals))
        for b in range(8):
            prefix[k + 1, b] = totals[b]
        return totals

    lax.fori_loop(0, slots, add_slot, (zero,) * 8, unroll=4)

    def place_row(row, carry):
        lanes = pl.ds(pl.multiple_of(row * 128, 128), 128)
        for col in range(tcols):
            p = col * trows + row
            first = plan_smem[1, p]
            last = plan_smem[1, p + 1]
            for b in range(8):
                v = prefix[last, b] - prefix[first, b]
                both = jnp.concatenate([v & 0xFFFF, v >> 16], axis=0)
                at_ref[pl.ds(col * 128 + b * 16, 16), lanes] = both.astype(F32).astype(BF16)
        return carry

    lax.fori_loop(0, trows, place_row, 0)

    for i in range(1, n_row):
        arrive(feats, feat_r, (r + i) % n_row)

    def forward(q):
        lanes = pl.ds(pl.multiple_of(q * n, n), n)
        total = dot(feats[0], at_ref[pl.ds(0, n), lanes])
        for k in range(1, n_row):
            total += dot(feats[k], at_ref[pl.ds(k * n, n), lanes])
        part[q] = total.astype(BF16)

    def pair_copy(zz):
        q = zz * 2 + 1 - core
        return copy_to(part.at[q], pair.at[zz], pair_s.at[zz], pair_r.at[zz], sibling)

    @pl.loop(1, n_z + 1)
    def _(i):
        zz = (z + i) % n_z
        forward(zz * 2 + 1 - core)
        pair_copy(zz).start()

    @pl.loop(1, n_z + 1)
    def _(i):
        forward(((z + i) % n_z) * 2 + core)

    def sum_copy(i):
        zz = (z + i) % n_z
        return copy_to(
            sums.at[zz], arrived.at[z], sum_s.at[zz], sum_r.at[z], (r, zz * 2 + core)
        )

    @pl.loop(1, n_z)
    def _(i):
        zz = (z + i) % n_z
        arrive(pair, pair_r, zz)
        sums[zz] = (part[zz * 2 + core].astype(F32) + pair[zz].astype(F32)).astype(BF16)
        sum_copy(i).start()

    for i in range(1, n_z):
        q = ((z + i) % n_z) * 2 + core
        arrive(grads, grad_r, q)
        relay_copy(q).start()
    for i in range(n_z):
        arrive(grads, grad_r, ((z + i) % n_z) * 2 + 1 - core)

    def back_copy(q):
        return copy_to(back.at[q], back_in.at[r], back_s.at[q], back_r.at[r], (q, c))

    def backward(q):
        rows = pl.ds(pl.multiple_of(q * n, n), n)
        back[q] = dot(at_ref[rows, :], grads[...].reshape(n_col * n, -1)).astype(BF16)

    @pl.loop(1, n_row)
    def _(i):
        q = (r + i) % n_row
        backward(q)
        back_copy(q).start()

    local = dot(part[0], grads[0])
    for q in range(1, n_col):
        local += dot(part[q], grads[q])
    rounded = local.astype(BF16)
    slab = rounded.shape[0] // n_plane
    for d in range(n_plane):
        w_part[d] = rounded[d * slab : (d + 1) * slab]

    def w1_copy(i):
        q, device = plane_peer(i)
        return copy_to(w_part.at[q], w_in.at[me], w1_s.at[q], w1_r.at[me], device)

    def w2_copy(i):
        q, device = z_peer(i)
        return copy_to(w_mid.at[z], w_mid.at[z], w2_s.at[q], w2_r.at[z], device)

    def w3_copy(i):
        q, device = plane_peer(i)
        return copy_to(w_all.at[me], w_all.at[me], w3_s.at[q], w3_r.at[me], device)

    for i in range(1, n_plane):
        w1_copy(i).start()
    backward(r)
    w_in[me] = w_part[me]
    for i in range(1, n_plane):
        arrive(w_in, w1_r, (me + i) % n_plane)
    w_mid[z] = jnp.sum(w_in[...].astype(F32), axis=0).astype(BF16)
    for i in range(1, n_z):
        w2_copy(i).start()

    loads[3].wait()
    total = back[r].astype(F32)
    for i in range(1, n_row):
        q = (r + i) % n_row
        arrive(back_in, back_r, q)
        total += back_in[q].astype(F32)
    ordered = dot(order, total.astype(BF16)).astype(BF16)
    igrad_ref[...] = dot(ordered, weight_ref[...], ((1,), (1,))).astype(BF16)

    for i in range(1, n_z):
        arrive(w_mid, w2_r, (z + i) % n_z)
    w_all[me] = jnp.sum(w_mid[...].astype(F32), axis=0).astype(BF16)
    for i in range(1, n_plane):
        w3_copy(i).start()

    arrive(pair, pair_r, z)
    total = part[c].astype(F32) + pair[z].astype(F32)
    for i in range(1, n_z):
        zz = (z + i) % n_z
        arrive(arrived, sum_r, zz)
        total += arrived[zz].astype(F32)
    out_ref[...] = dot((total / deg_row).astype(BF16), weight_ref[...], ((0,), (0,))).astype(BF16)

    for i in range(1, n_plane):
        arrive(w_all, w3_r, (me + i) % n_plane)
    for d in range(n_plane):
        wgrad_ref[d * slab : (d + 1) * slab, :] = w_all[d].astype(F32)

    for i in range(1, n_row):
        feat_copy(i)[1].wait_send()
        back_copy((r + i) % n_row).wait_send()
    for i in range(1, n_z):
        grad_copy(i)[1].wait_send()
        sum_copy(i).wait_send()
    for i in range(n_z):
        zz = (z + i) % n_z
        relay_copy(zz * 2 + core).wait_send()
        pair_copy(zz).wait_send()

    for i in range(1, n_plane):
        w1_copy(i).wait_send()
        w3_copy(i).wait_send()
    for i in range(1, n_z):
        w2_copy(i).wait_send()


def layer(rows, cols, count, bits, features, cotangent, degrees, weight, n_row, n_z):
    n, width = features.shape
    n_col = 2 * n_z
    n_plane = 2 * n_row
    slots = bits.shape[0]
    block = lambda k: pltpu.VMEM((k, n, width), BF16)
    sems = lambda k: pltpu.SemaphoreType.DMA((k,))
    slab = lambda k: pltpu.VMEM((k, width // n_plane, width), BF16)
    tile = jax.ShapeDtypeStruct((n, width), BF16)
    return pl.pallas_call(
        functools.partial(layer_kernel, n_row, n_z),
        out_shape=(tile, jax.ShapeDtypeStruct((width, width), F32), tile),
        in_specs=[pl.BlockSpec(memory_space=VMEM)] * 4 + [pl.BlockSpec(memory_space=pl.ANY)] * 4,
        out_specs=(pl.BlockSpec(memory_space=VMEM),) * 3,
        scratch_shapes=[
            pltpu.VMEM((n * n_row, n * n_col), BF16),
            pltpu.VMEM((slots + 1, 8, 8, 128), jnp.int32),
            pltpu.VMEM((2, slots), jnp.int32),
            pltpu.SMEM((2, slots), jnp.int32),
            pltpu.VMEM(bits.shape, jnp.int32),
            pltpu.VMEM((n, width), BF16),
            pltpu.VMEM((n, width), BF16),
            pltpu.VMEM((width, width), BF16),
            sems(4), pltpu.SemaphoreType.DMA,
            block(n_row), block(n_col), block(n_col), block(n_z), block(n_z), block(n_z),
            block(n_row), block(n_row), slab(n_plane), slab(n_plane), slab(n_z), slab(n_plane),
            sems(n_row), sems(n_row), sems(n_col), sems(n_col), sems(n_z), sems(n_z), sems(n_z),
            sems(n_z), sems(n_z), sems(n_row), sems(n_row),
            sems(n_plane), sems(n_plane), sems(n_z), sems(n_z), sems(n_plane), sems(n_plane),
        ],
        compiler_params=pltpu.CompilerParams(
            collective_id=0, has_side_effects=True, vmem_limit_bytes=48 * 2**20
        ),
        name="layer",
    )(rows, cols, count, degrees, bits, features, cotangent, weight)


def swap_order(x, a, b):
    return x.reshape(-1, a, b, x.shape[-1]).swapaxes(1, 2).reshape(x.shape)


def per_device(features, cotangent, degrees, weight, tile_rows, tile_cols, tile_bits, tile_count):
    nodes, width = features.shape
    trows = nodes * lax.axis_size("col") // 128
    tcols = nodes * lax.axis_size("row") // 128
    n_row, n_col = lax.axis_size("row"), lax.axis_size("col")
    slots = tile_bits.shape[2]
    if n_row * n_col == 32 and nodes == width and trows * tcols < slots:
        return layer(
            tile_rows[0], tile_cols[0], tile_count, tile_bits[0, 0],
            features, cotangent, degrees.reshape(1, nodes), weight, n_row, n_col // 2,
        )
    at = build_adjacency(
        tile_count[0], tile_rows[0, 0], tile_cols[0, 0], tile_bits[0, 0], trows, tcols
    )
    deg = degrees[:, None].astype(F32)
    scaled = (cotangent.astype(F32) / deg).astype(BF16)
    feats = lax.all_gather(swap_order(features, 16, 8), "row", axis=0, tiled=True)
    grads = lax.all_gather(scaled, "col", axis=0, tiled=True)
    fwd = lax.dot_general(at, feats, (((0,), (0,)), ((), ())), preferred_element_type=F32)
    fwd = fwd.astype(BF16)
    local = lax.dot_general(fwd, grads, (((0,), (0,)), ((), ())), preferred_element_type=F32)
    weight_grad = lax.psum(local, ("row", "col"))
    summed = lax.psum_scatter(fwd, "col", scatter_dimension=0, tiled=True).astype(F32)
    aggregated = (summed / deg).astype(BF16)
    output = jnp.dot(aggregated, weight, preferred_element_type=F32).astype(BF16)
    bwd = jnp.dot(at, grads, preferred_element_type=F32).astype(BF16)
    back = swap_order(lax.psum_scatter(bwd, "row", scatter_dimension=0, tiled=True), 8, 16)
    input_grad = jnp.dot(back, weight.T, preferred_element_type=F32).astype(BF16)
    return output, weight_grad, input_grad


def solution(mesh):
    placed = (
        P(("col", "row"), None),
        P(("row", "col"), None),
        P(("row", "col")),
        P(),
        P("row", "col", None),
        P("row", "col", None),
        P("row", "col", None, None, None),
        P("row", "col"),
    )
    return jax.shard_map(
        per_device,
        mesh=mesh,
        in_specs=placed,
        out_specs=(P(("row", "col"), None), P(), P(("col", "row"), None)),
        check_vma=False,
    )
```

```python
import functools

import jax
import jax.numpy as jnp
from jax import lax
from jax.experimental import pallas as pl
from jax.experimental.pallas import tpu as pltpu
from jax.sharding import PartitionSpec as P

SMEM = pltpu.SMEM
VMEM = pltpu.VMEM
BF16 = jnp.bfloat16
F32 = jnp.float32


def build_kernel(trows, chunk, count_ref, rows_ref, cols_ref, bits_ref, out_ref, acc0, acc1):
    base = pl.program_id(0) * chunk
    zero = jnp.zeros(acc0.shape[1:], jnp.int32)

    def clear(p, carry):
        acc0[p] = zero
        acc1[p] = zero
        return carry

    lax.fori_loop(0, chunk * trows, clear, 0, unroll=4)
    count = count_ref[0]

    def add_pair(k, carry):
        for half, acc in enumerate((acc0, acc1)):
            s = 2 * k + half
            col = cols_ref[s] - base
            ok = (s < count) & (col >= 0) & (col < chunk)
            p = jnp.where(ok, col * trows + rows_ref[s], 0)
            words = bits_ref[s]
            word = (words[:8] | (words[8:] << 16)) & (0 - ok.astype(jnp.int32))
            for b in range(8):
                acc[p, b] += (word >> b) & 0x10001
        return carry

    lax.fori_loop(0, (count + 1) // 2, add_pair, 0)

    def convert(row, carry):
        lanes = pl.ds(pl.multiple_of(row * 128, 128), 128)
        for col in range(chunk):
            p = col * trows + row
            for b in range(8):
                v = acc0[p, b] + acc1[p, b]
                both = jnp.concatenate([v & 0xFFFF, v >> 16], axis=0)
                out_ref[pl.ds(col * 128 + b * 16, 16), lanes] = both.astype(F32).astype(BF16)
        return carry

    lax.fori_loop(0, trows, convert, 0)


def build_adjacency(count, rows, cols, bits, trows, tcols):
    chunk = max(d for d in range(1, tcols + 1) if tcols % d == 0 and d * trows <= 128)
    scratch = pltpu.VMEM((chunk * trows, 8, 8, 128), jnp.int32)
    return pl.pallas_call(
        functools.partial(build_kernel, trows, chunk),
        grid=(tcols // chunk,),
        out_shape=jax.ShapeDtypeStruct((tcols * 128, trows * 128), BF16),
        in_specs=[
            pl.BlockSpec(memory_space=SMEM),
            pl.BlockSpec(memory_space=SMEM),
            pl.BlockSpec(memory_space=SMEM),
            pl.BlockSpec(memory_space=VMEM),
        ],
        out_specs=pl.BlockSpec((chunk * 128, trows * 128), lambda g: (g, 0)),
        scratch_shapes=[scratch, scratch],
        compiler_params=pltpu.CompilerParams(vmem_limit_bytes=40 * 2**20),
        name="build_adjacency",
    )(count, rows, cols, bits)


MESH = pl.DeviceIdType.MESH


def copy_to(src, dst, send_sem, recv_sem, device):
    return pltpu.make_async_remote_copy(
        src_ref=src,
        dst_ref=dst,
        send_sem=send_sem,
        recv_sem=recv_sem,
        device_id=device,
        device_id_type=MESH,
    )


def dot(a, b, dims=((1,), (0,))):
    return lax.dot_general(a, b, (dims, ((), ())), preferred_element_type=F32)


def layer_kernel(
    n_row, n_z,
    rows_ref, cols_ref, count_ref, deg_ref, bits_hbm, feat_hbm, cot_hbm, weight_hbm,
    out_ref, wgrad_ref, igrad_ref,
    at_ref, prefix, plan, plan_smem, bits_ref, feat_ref, cot_ref, weight_ref, load_s, plan_s,
    feats, grads, part, pair, sums, passed, arrived, back, back_in, w_part, w_in, w_mid, w_all,
    feat_s, feat_r, grad_s, grad_r, relay_s, on_s, pair_s, pair_r, sum_s, sum_r, pass_r, back_s, back_r,
    w1_s, w1_r, w2_s, w2_r, w3_s, w3_r,
):
    n = feat_ref.shape[0]
    n_col = 2 * n_z
    n_plane = n_row * 2
    r = lax.axis_index("row")
    c = lax.axis_index("col")
    z = c // 2
    core = c % 2
    sibling = (r, z * 2 + 1 - core)

    me = r * 2 + core

    def plane_peer(i):
        q = (me + i) % n_plane
        return q, (q // 2, z * 2 + q % 2)

    def z_peer(i):
        zz = (z + i) % n_z
        return zz, (r, zz * 2 + core)

    def flip(i):
        return ((z // 2 + i // 2) % 2) * 2 + (z + i) % 2

    mate = flip(1)
    inner = z % 2 != z // 2
    end = z % 2 == z // 2

    def at_z(zz):
        return (r, zz * 2 + core)

    barrier = pltpu.get_barrier_semaphore()
    for i in range(1, n_plane):
        pl.semaphore_signal(barrier, inc=1, device_id=plane_peer(i)[1], device_id_type=MESH)
    for i in range(1, n_z):
        pl.semaphore_signal(barrier, inc=1, device_id=z_peer(i)[1], device_id_type=MESH)
    loads = [
        pltpu.make_async_copy(src, dst, load_s.at[k])
        for k, (src, dst) in enumerate(
            ((cot_hbm, cot_ref), (feat_hbm, feat_ref), (bits_hbm, bits_ref), (weight_hbm, weight_ref))
        )
    ]
    for load in loads:
        load.start()

    i0 = lax.broadcasted_iota(jnp.int32, (n, n), 0)
    i1 = lax.broadcasted_iota(jnp.int32, (n, n), 1)
    placed = (i1 // 128) * 128 + (i1 % 16) * 8 + (i1 % 128) // 16
    order = (i0 == placed).astype(F32).astype(BF16)
    deg_row = deg_ref[...].astype(F32)
    deg_col = jnp.sum(jnp.where(i0 == i1, deg_row, 0.0), axis=1, keepdims=True)

    trows = n * n_col // 128
    tcols = n * n_row // 128
    places = trows * tcols
    slots = rows_ref.shape[1]
    s0 = lax.broadcasted_iota(jnp.int32, (slots, slots), 0)
    s1 = lax.broadcasted_iota(jnp.int32, (slots, slots), 1)
    lane = lax.broadcasted_iota(jnp.int32, (1, slots), 1)
    place = jnp.where(lane < count_ref[...], cols_ref[...] * trows + rows_ref[...], places)
    key_row = (place * slots + lane).astype(F32)
    key_col = jnp.sum(jnp.where(s0 == s1, key_row, 0.0), axis=1, keepdims=True)
    rank = jnp.sum((key_row < key_col).astype(F32), axis=1, keepdims=True)
    picked = jnp.where(rank == s1.astype(F32), s0, 0)
    before = (key_col < (s1 * slots).astype(F32)).astype(jnp.int32)
    plan[0:1, :] = jnp.clip(jnp.sum(picked, axis=0, keepdims=True), 0, slots - 1)
    plan[1:2, :] = jnp.clip(jnp.sum(before, axis=0, keepdims=True), 0, slots)
    plan_copy = pltpu.make_async_copy(plan, plan_smem, plan_s)
    plan_copy.start()

    loads[0].wait()
    loads[1].wait()
    grads[c] = (cot_ref[...].astype(F32) / deg_col).astype(BF16)
    feats[r] = dot(feat_ref[...], order, ((0,), (0,))).astype(BF16)

    pl.semaphore_wait(barrier, n_plane + n_z - 2)

    def feat_copy(i):
        q = (r + i) % n_row
        return q, copy_to(feats.at[r], feats.at[r], feat_s.at[q], feat_r.at[r], (q, c))

    def grad_copy(k):
        zz = (2 - z // 2, mate)[k]
        return copy_to(grads.at[c], grads.at[c], grad_s.at[k], grad_r.at[c], at_z(zz))

    def on_copy(i):
        q = flip(i) * 2 + core
        return copy_to(grads.at[q], grads.at[q], on_s.at[i], grad_r.at[q], at_z(mate))

    def relay_copy(q):
        return copy_to(grads.at[q], grads.at[q], relay_s.at[q // 2], grad_r.at[q], sibling)

    for i in range(1, n_row):
        feat_copy(i)[1].start()
    for k in range(2):
        grad_copy(k).start()
    relay_copy(c).start()

    def arrive(ref, sem, slot):
        copy_to(ref.at[slot], ref.at[slot], sem.at[slot], sem.at[slot], sibling).wait_recv()

    plan_copy.wait()
    loads[2].wait()
    zero = jnp.zeros((8, 128), jnp.int32)
    for b in range(8):
        prefix[0, b] = zero

    def add_slot(k, totals):
        words = bits_ref[plan_smem[0, k]]
        word = words[:8] | (words[8:] << 16)
        totals = tuple(t + ((word >> b) & 0x10001) for b, t in enumerate(totals))
        for b in range(8):
            prefix[k + 1, b] = totals[b]
        return totals

    lax.fori_loop(0, slots, add_slot, (zero,) * 8, unroll=4)

    def place_row(row, carry):
        lanes = pl.ds(pl.multiple_of(row * 128, 128), 128)
        for col in range(tcols):
            p = col * trows + row
            first = plan_smem[1, p]
            last = plan_smem[1, p + 1]
            for b in range(8):
                v = prefix[last, b] - prefix[first, b]
                both = jnp.concatenate([v & 0xFFFF, v >> 16], axis=0)
                at_ref[pl.ds(col * 128 + b * 16, 16), lanes] = both.astype(F32).astype(BF16)
        return carry

    lax.fori_loop(0, trows, place_row, 0)

    @pl.when(inner)
    def _():
        for i in (3, 2):
            q = flip(i) * 2 + core
            arrive(grads, grad_r, q)
            on_copy(i).start()
            relay_copy(q).start()

    for i in range(1, n_row):
        arrive(feats, feat_r, (r + i) % n_row)

    def forward(q):
        lanes = pl.ds(pl.multiple_of(q * n, n), n)
        total = dot(feats[0], at_ref[pl.ds(0, n), lanes])
        for k in range(1, n_row):
            total += dot(feats[k], at_ref[pl.ds(k * n, n), lanes])
        part[q] = total.astype(BF16)

    def pair_copy(zz):
        q = zz * 2 + 1 - core
        return copy_to(part.at[q], pair.at[zz], pair_s.at[zz], pair_r.at[zz], sibling)

    @pl.loop(0, n_z)
    def _(i):
        zz = flip(3 - i)
        forward(zz * 2 + 1 - core)
        pair_copy(zz).start()

    @pl.loop(0, n_z)
    def _(i):
        forward(flip(3 - i) * 2 + core)

    def paired(zz):
        arrive(pair, pair_r, zz)
        return part[zz * 2 + core].astype(F32) + pair[zz].astype(F32)

    def pass_copy(i):
        zz = flip(i)
        return copy_to(sums.at[zz], passed.at[zz], sum_s.at[zz], pass_r.at[zz], at_z(mate))

    def sum_copy(i):
        zz = flip(i)
        k = 0 if i == 1 else 1
        return copy_to(sums.at[zz], arrived.at[k], sum_s.at[zz], sum_r.at[k], at_z(zz))

    @pl.when(end)
    def _():
        for i in (3, 2):
            sums[flip(i)] = paired(flip(i)).astype(BF16)
            pass_copy(i).start()

    sums[mate] = paired(mate).astype(BF16)
    sum_copy(1).start()

    arrive(grads, grad_r, mate * 2 + core)
    relay_copy(mate * 2 + core).start()

    @pl.when(end)
    def _():
        for i in (2, 3):
            q = flip(i) * 2 + core
            arrive(grads, grad_r, q)
            relay_copy(q).start()

    for i in range(n_z):
        arrive(grads, grad_r, flip(i) * 2 + 1 - core)

    def back_copy(q):
        return copy_to(back.at[q], back_in.at[r], back_s.at[q], back_r.at[r], (q, c))

    def backward(q):
        rows = pl.ds(pl.multiple_of(q * n, n), n)
        back[q] = dot(at_ref[rows, :], grads[...].reshape(n_col * n, -1)).astype(BF16)

    @pl.loop(1, n_row)
    def _(i):
        q = (r + i) % n_row
        backward(q)
        back_copy(q).start()

    @pl.when(inner)
    def _():
        for i in (2, 3):
            zz = flip(i)
            total = paired(zz)
            arrive(passed, pass_r, zz)
            sums[zz] = (total + passed[zz].astype(F32)).astype(BF16)
            sum_copy(i).start()

    local = dot(part[0], grads[0])
    for q in range(1, n_col):
        local += dot(part[q], grads[q])
    rounded = local.astype(BF16)
    slab = rounded.shape[0] // n_plane
    for d in range(n_plane):
        w_part[d] = rounded[d * slab : (d + 1) * slab]

    def w1_copy(i):
        q, device = plane_peer(i)
        return copy_to(w_part.at[q], w_in.at[me], w1_s.at[q], w1_r.at[me], device)

    def w2_copy(i):
        q, device = z_peer(i)
        return copy_to(w_mid.at[z], w_mid.at[z], w2_s.at[q], w2_r.at[z], device)

    def w3_copy(i):
        q, device = plane_peer(i)
        return copy_to(w_all.at[me], w_all.at[me], w3_s.at[q], w3_r.at[me], device)

    for i in range(1, n_plane):
        w1_copy(i).start()
    backward(r)
    w_in[me] = w_part[me]
    for i in range(1, n_plane):
        arrive(w_in, w1_r, (me + i) % n_plane)
    w_mid[z] = jnp.sum(w_in[...].astype(F32), axis=0).astype(BF16)
    for i in range(1, n_z):
        w2_copy(i).start()

    loads[3].wait()
    total = back[r].astype(F32)
    for i in range(1, n_row):
        q = (r + i) % n_row
        arrive(back_in, back_r, q)
        total += back_in[q].astype(F32)
    ordered = dot(order, total.astype(BF16)).astype(BF16)
    igrad_ref[...] = dot(ordered, weight_ref[...], ((1,), (1,))).astype(BF16)

    for i in range(1, n_z):
        arrive(w_mid, w2_r, (z + i) % n_z)
    w_all[me] = jnp.sum(w_mid[...].astype(F32), axis=0).astype(BF16)
    for i in range(1, n_plane):
        w3_copy(i).start()

    total = paired(z)
    for k in range(2):
        arrive(arrived, sum_r, k)
        total += arrived[k].astype(F32)
    out_ref[...] = dot((total / deg_row).astype(BF16), weight_ref[...], ((0,), (0,))).astype(BF16)

    for i in range(1, n_plane):
        arrive(w_all, w3_r, (me + i) % n_plane)
    for d in range(n_plane):
        wgrad_ref[d * slab : (d + 1) * slab, :] = w_all[d].astype(F32)

    for i in range(1, n_row):
        feat_copy(i)[1].wait_send()
        back_copy((r + i) % n_row).wait_send()
    for k in range(2):
        grad_copy(k).wait_send()
    sum_copy(1).wait_send()

    @pl.when(inner)
    def _():
        for i in (2, 3):
            on_copy(i).wait_send()
            sum_copy(i).wait_send()

    @pl.when(end)
    def _():
        for i in (2, 3):
            pass_copy(i).wait_send()

    for i in range(n_z):
        zz = (z + i) % n_z
        relay_copy(zz * 2 + core).wait_send()
        pair_copy(zz).wait_send()

    for i in range(1, n_plane):
        w1_copy(i).wait_send()
        w3_copy(i).wait_send()
    for i in range(1, n_z):
        w2_copy(i).wait_send()


def layer(rows, cols, count, bits, features, cotangent, degrees, weight, n_row, n_z):
    n, width = features.shape
    n_col = 2 * n_z
    n_plane = 2 * n_row
    slots = bits.shape[0]
    block = lambda k: pltpu.VMEM((k, n, width), BF16)
    sems = lambda k: pltpu.SemaphoreType.DMA((k,))
    slab = lambda k: pltpu.VMEM((k, width // n_plane, width), BF16)
    tile = jax.ShapeDtypeStruct((n, width), BF16)
    return pl.pallas_call(
        functools.partial(layer_kernel, n_row, n_z),
        out_shape=(tile, jax.ShapeDtypeStruct((width, width), F32), tile),
        in_specs=[pl.BlockSpec(memory_space=VMEM)] * 4 + [pl.BlockSpec(memory_space=pl.ANY)] * 4,
        out_specs=(pl.BlockSpec(memory_space=VMEM),) * 3,
        scratch_shapes=[
            pltpu.VMEM((n * n_row, n * n_col), BF16),
            pltpu.VMEM((slots + 1, 8, 8, 128), jnp.int32),
            pltpu.VMEM((2, slots), jnp.int32),
            pltpu.SMEM((2, slots), jnp.int32),
            pltpu.VMEM(bits.shape, jnp.int32),
            pltpu.VMEM((n, width), BF16),
            pltpu.VMEM((n, width), BF16),
            pltpu.VMEM((width, width), BF16),
            sems(4), pltpu.SemaphoreType.DMA,
            block(n_row), block(n_col), block(n_col), block(n_z), block(n_z), block(n_z), block(2),
            block(n_row), block(n_row), slab(n_plane), slab(n_plane), slab(n_z), slab(n_plane),
            sems(n_row), sems(n_row), sems(2), sems(n_col), sems(n_z), sems(4), sems(n_z), sems(n_z),
            sems(n_z), sems(2), sems(n_z), sems(n_row), sems(n_row),
            sems(n_plane), sems(n_plane), sems(n_z), sems(n_z), sems(n_plane), sems(n_plane),
        ],
        compiler_params=pltpu.CompilerParams(
            collective_id=0, has_side_effects=True, vmem_limit_bytes=64 * 2**20
        ),
        name="layer",
    )(rows, cols, count, degrees, bits, features, cotangent, weight)


def swap_order(x, a, b):
    return x.reshape(-1, a, b, x.shape[-1]).swapaxes(1, 2).reshape(x.shape)


def per_device(features, cotangent, degrees, weight, tile_rows, tile_cols, tile_bits, tile_count):
    nodes, width = features.shape
    trows = nodes * lax.axis_size("col") // 128
    tcols = nodes * lax.axis_size("row") // 128
    n_row, n_col = lax.axis_size("row"), lax.axis_size("col")
    slots = tile_bits.shape[2]
    if n_row == 4 and n_col == 8 and nodes == width and trows * tcols < slots:
        return layer(
            tile_rows[0], tile_cols[0], tile_count, tile_bits[0, 0],
            features, cotangent, degrees.reshape(1, nodes), weight, n_row, n_col // 2,
        )
    at = build_adjacency(
        tile_count[0], tile_rows[0, 0], tile_cols[0, 0], tile_bits[0, 0], trows, tcols
    )
    deg = degrees[:, None].astype(F32)
    scaled = (cotangent.astype(F32) / deg).astype(BF16)
    feats = lax.all_gather(swap_order(features, 16, 8), "row", axis=0, tiled=True)
    grads = lax.all_gather(scaled, "col", axis=0, tiled=True)
    fwd = lax.dot_general(at, feats, (((0,), (0,)), ((), ())), preferred_element_type=F32)
    fwd = fwd.astype(BF16)
    local = lax.dot_general(fwd, grads, (((0,), (0,)), ((), ())), preferred_element_type=F32)
    weight_grad = lax.psum(local, ("row", "col"))
    summed = lax.psum_scatter(fwd, "col", scatter_dimension=0, tiled=True).astype(F32)
    aggregated = (summed / deg).astype(BF16)
    output = jnp.dot(aggregated, weight, preferred_element_type=F32).astype(BF16)
    bwd = jnp.dot(at, grads, preferred_element_type=F32).astype(BF16)
    back = swap_order(lax.psum_scatter(bwd, "row", scatter_dimension=0, tiled=True), 8, 16)
    input_grad = jnp.dot(back, weight.T, preferred_element_type=F32).astype(BF16)
    return output, weight_grad, input_grad


def solution(mesh):
    placed = (
        P(("col", "row"), None),
        P(("row", "col"), None),
        P(("row", "col")),
        P(),
        P("row", "col", None),
        P("row", "col", None),
        P("row", "col", None, None, None),
        P("row", "col"),
    )
    return jax.shard_map(
        per_device,
        mesh=mesh,
        in_specs=placed,
        out_specs=(P(("row", "col"), None), P(), P(("col", "row"), None)),
        check_vma=False,
    )
```

```python
import functools

import jax
import jax.numpy as jnp
from jax import lax
from jax.experimental import pallas as pl
from jax.experimental.pallas import tpu as pltpu
from jax.sharding import PartitionSpec as P

SMEM = pltpu.SMEM
VMEM = pltpu.VMEM
BF16 = jnp.bfloat16
F32 = jnp.float32


def build_kernel(trows, chunk, count_ref, rows_ref, cols_ref, bits_ref, out_ref, acc0, acc1):
    base = pl.program_id(0) * chunk
    zero = jnp.zeros(acc0.shape[1:], jnp.int32)

    def clear(p, carry):
        acc0[p] = zero
        acc1[p] = zero
        return carry

    lax.fori_loop(0, chunk * trows, clear, 0, unroll=4)
    count = count_ref[0]

    def add_pair(k, carry):
        for half, acc in enumerate((acc0, acc1)):
            s = 2 * k + half
            col = cols_ref[s] - base
            ok = (s < count) & (col >= 0) & (col < chunk)
            p = jnp.where(ok, col * trows + rows_ref[s], 0)
            words = bits_ref[s]
            word = (words[:8] | (words[8:] << 16)) & (0 - ok.astype(jnp.int32))
            for b in range(8):
                acc[p, b] += (word >> b) & 0x10001
        return carry

    lax.fori_loop(0, (count + 1) // 2, add_pair, 0)

    def convert(row, carry):
        lanes = pl.ds(pl.multiple_of(row * 128, 128), 128)
        for col in range(chunk):
            p = col * trows + row
            for b in range(8):
                v = acc0[p, b] + acc1[p, b]
                both = jnp.concatenate([v & 0xFFFF, v >> 16], axis=0)
                out_ref[pl.ds(col * 128 + b * 16, 16), lanes] = both.astype(F32).astype(BF16)
        return carry

    lax.fori_loop(0, trows, convert, 0)


def build_adjacency(count, rows, cols, bits, trows, tcols):
    chunk = max(d for d in range(1, tcols + 1) if tcols % d == 0 and d * trows <= 128)
    scratch = pltpu.VMEM((chunk * trows, 8, 8, 128), jnp.int32)
    return pl.pallas_call(
        functools.partial(build_kernel, trows, chunk),
        grid=(tcols // chunk,),
        out_shape=jax.ShapeDtypeStruct((tcols * 128, trows * 128), BF16),
        in_specs=[
            pl.BlockSpec(memory_space=SMEM),
            pl.BlockSpec(memory_space=SMEM),
            pl.BlockSpec(memory_space=SMEM),
            pl.BlockSpec(memory_space=VMEM),
        ],
        out_specs=pl.BlockSpec((chunk * 128, trows * 128), lambda g: (g, 0)),
        scratch_shapes=[scratch, scratch],
        compiler_params=pltpu.CompilerParams(vmem_limit_bytes=40 * 2**20),
        name="build_adjacency",
    )(count, rows, cols, bits)


MESH = pl.DeviceIdType.MESH


def copy_to(src, dst, send_sem, recv_sem, device):
    return pltpu.make_async_remote_copy(
        src_ref=src,
        dst_ref=dst,
        send_sem=send_sem,
        recv_sem=recv_sem,
        device_id=device,
        device_id_type=MESH,
    )


def dot(a, b, dims=((1,), (0,))):
    return lax.dot_general(a, b, (dims, ((), ())), preferred_element_type=F32)


def layer_kernel(
    n_row, n_z,
    count_ref, rows_hbm, cols_hbm, deg_hbm, bits_hbm, feat_hbm, cot_hbm, weight_hbm,
    out_ref, wgrad_ref, igrad_ref,
    at_ref, prefix, plan, plan_smem, rows_ref, cols_ref, deg_ref, bits_ref, feat_ref, cot_ref, weight_ref, load_s, plan_s,
    feats, grads, part, pair, sums, passed, arrived, back, back_in, w_part, w_in, w_mid, w_all,
    feat_s, feat_r, grad_s, grad_r, relay_s, pair_s, pair_r, sum_s, sum_r, pass_r, back_s, back_r,
    w1_s, w1_r, w2_s, w2_r, w3_s, w3_r,
):
    n = feat_ref.shape[0]
    n_col = 2 * n_z
    n_plane = n_row * 2
    r = lax.axis_index("row")
    c = lax.axis_index("col")
    z = c // 2
    core = c % 2
    sibling = (r, z * 2 + 1 - core)

    me = r * 2 + core

    def plane_peer(i):
        q = (me + i) % n_plane
        return q, (q // 2, z * 2 + q % 2)

    def z_peer(i):
        zz = (z + i) % n_z
        return zz, (r, zz * 2 + core)

    def flip(i):
        return ((z // 2 + i // 2) % 2) * 2 + (z + i) % 2

    mate = flip(1)
    inner = z % 2 != z // 2
    end = z % 2 == z // 2

    def at_z(zz):
        return (r, zz * 2 + core)

    barrier = pltpu.get_barrier_semaphore()
    for i in range(1, n_plane):
        pl.semaphore_signal(barrier, inc=1, device_id=plane_peer(i)[1], device_id_type=MESH)
    for i in range(1, n_z):
        pl.semaphore_signal(barrier, inc=1, device_id=z_peer(i)[1], device_id_type=MESH)
    loads = [
        pltpu.make_async_copy(src, dst, load_s.at[k])
        for k, (src, dst) in enumerate(
            (
                (rows_hbm, rows_ref), (cols_hbm, cols_ref), (deg_hbm, deg_ref), (cot_hbm, cot_ref),
                (feat_hbm, feat_ref), (bits_hbm, bits_ref), (weight_hbm, weight_ref),
            )
        )
    ]
    for load in loads:
        load.start()

    i0 = lax.broadcasted_iota(jnp.int32, (n, n), 0)
    i1 = lax.broadcasted_iota(jnp.int32, (n, n), 1)
    placed = (i1 // 128) * 128 + (i1 % 16) * 8 + (i1 % 128) // 16
    order = (i0 == placed).astype(F32).astype(BF16)
    for load in loads[:3]:
        load.wait()
    deg_row = deg_ref[...].astype(F32)
    deg_col = jnp.sum(jnp.where(i0 == i1, deg_row, 0.0), axis=1, keepdims=True)

    trows = n * n_col // 128
    tcols = n * n_row // 128
    places = trows * tcols
    slots = rows_ref.shape[1]
    s0 = lax.broadcasted_iota(jnp.int32, (slots, slots), 0)
    s1 = lax.broadcasted_iota(jnp.int32, (slots, slots), 1)
    lane = lax.broadcasted_iota(jnp.int32, (1, slots), 1)
    place = jnp.where(lane < count_ref[...], cols_ref[...] * trows + rows_ref[...], places)
    key_row = (place * slots + lane).astype(F32)
    key_col = jnp.sum(jnp.where(s0 == s1, key_row, 0.0), axis=1, keepdims=True)
    rank = jnp.sum((key_row < key_col).astype(F32), axis=1, keepdims=True)
    picked = jnp.where(rank == s1.astype(F32), s0, 0)
    before = (key_col < (s1 * slots).astype(F32)).astype(jnp.int32)
    plan[0:1, :] = jnp.clip(jnp.sum(picked, axis=0, keepdims=True), 0, slots - 1)
    plan[1:2, :] = jnp.clip(jnp.sum(before, axis=0, keepdims=True), 0, slots)
    plan_copy = pltpu.make_async_copy(plan, plan_smem, plan_s)
    plan_copy.start()

    loads[3].wait()
    loads[4].wait()
    grads[c] = (cot_ref[...].astype(F32) / deg_col).astype(BF16)
    feats[r] = dot(feat_ref[...], order, ((0,), (0,))).astype(BF16)

    pl.semaphore_wait(barrier, n_plane + n_z - 2)

    def feat_copy(i):
        q = (r + i) % n_row
        return q, copy_to(feats.at[r], feats.at[r], feat_s.at[q], feat_r.at[r], (q, c))

    def grad_copy(i):
        return copy_to(grads.at[c], grads.at[c], grad_s.at[i], grad_r.at[c], at_z(flip(i)))

    def relay_copy(q):
        return copy_to(grads.at[q], grads.at[q], relay_s.at[q // 2], grad_r.at[q], sibling)

    for i in range(1, n_row):
        feat_copy(i)[1].start()
    for i in (3, 2, 1):
        grad_copy(i).start()
    relay_copy(c).start()

    def arrive(ref, sem, slot):
        copy_to(ref.at[slot], ref.at[slot], sem.at[slot], sem.at[slot], sibling).wait_recv()

    plan_copy.wait()
    loads[5].wait()
    zero = jnp.zeros((8, 128), jnp.int32)
    for b in range(8):
        prefix[0, b] = zero

    def add_slot(k, totals):
        words = bits_ref[plan_smem[0, k]]
        word = words[:8] | (words[8:] << 16)
        totals = tuple(t + ((word >> b) & 0x10001) for b, t in enumerate(totals))
        for b in range(8):
            prefix[k + 1, b] = totals[b]
        return totals

    lax.fori_loop(0, slots, add_slot, (zero,) * 8, unroll=4)

    def place_row(row, carry):
        lanes = pl.ds(pl.multiple_of(row * 128, 128), 128)
        for col in range(tcols):
            p = col * trows + row
            first = plan_smem[1, p]
            last = plan_smem[1, p + 1]
            for b in range(8):
                v = prefix[last, b] - prefix[first, b]
                both = jnp.concatenate([v & 0xFFFF, v >> 16], axis=0)
                at_ref[pl.ds(col * 128 + b * 16, 16), lanes] = both.astype(F32).astype(BF16)
        return carry

    lax.fori_loop(0, trows, place_row, 0)

    for i in range(1, n_row):
        arrive(feats, feat_r, (r + i) % n_row)

    def forward(q):
        lanes = pl.ds(pl.multiple_of(q * n, n), n)
        total = dot(feats[0], at_ref[pl.ds(0, n), lanes])
        for k in range(1, n_row):
            total += dot(feats[k], at_ref[pl.ds(k * n, n), lanes])
        part[q] = total.astype(BF16)

    def pair_copy(zz):
        q = zz * 2 + 1 - core
        return copy_to(part.at[q], pair.at[zz], pair_s.at[zz], pair_r.at[zz], sibling)

    @pl.loop(0, n_z)
    def _(i):
        zz = flip(3 - i)
        forward(zz * 2 + 1 - core)
        pair_copy(zz).start()

    @pl.loop(0, n_z)
    def _(i):
        forward(flip(3 - i) * 2 + core)

    def paired(zz):
        arrive(pair, pair_r, zz)
        return part[zz * 2 + core].astype(F32) + pair[zz].astype(F32)

    def pass_copy(i):
        zz = flip(i)
        return copy_to(sums.at[zz], passed.at[zz], sum_s.at[zz], pass_r.at[zz], at_z(mate))

    def sum_copy(i):
        zz = flip(i)
        k = 0 if i == 1 else 1
        return copy_to(sums.at[zz], arrived.at[k], sum_s.at[zz], sum_r.at[k], at_z(zz))

    @pl.when(end)
    def _():
        for i in (3, 2):
            sums[flip(i)] = paired(flip(i)).astype(BF16)
            pass_copy(i).start()

    sums[mate] = paired(mate).astype(BF16)
    sum_copy(1).start()

    for i in (1, 2, 3):
        q = flip(i) * 2 + core
        arrive(grads, grad_r, q)
        relay_copy(q).start()

    for i in range(n_z):
        arrive(grads, grad_r, flip(i) * 2 + 1 - core)

    def back_copy(q):
        return copy_to(back.at[q], back_in.at[r], back_s.at[q], back_r.at[r], (q, c))

    def backward(q):
        rows = pl.ds(pl.multiple_of(q * n, n), n)
        back[q] = dot(at_ref[rows, :], grads[...].reshape(n_col * n, -1)).astype(BF16)

    @pl.loop(1, n_row)
    def _(i):
        q = (r + i) % n_row
        backward(q)
        back_copy(q).start()

    @pl.when(inner)
    def _():
        for i in (2, 3):
            zz = flip(i)
            total = paired(zz)
            arrive(passed, pass_r, zz)
            sums[zz] = (total + passed[zz].astype(F32)).astype(BF16)
            sum_copy(i).start()

    local = dot(part[0], grads[0])
    for q in range(1, n_col):
        local += dot(part[q], grads[q])
    rounded = local.astype(BF16)
    slab = rounded.shape[0] // n_plane
    for d in range(n_plane):
        w_part[d] = rounded[d * slab : (d + 1) * slab]

    def w1_copy(i):
        q, device = plane_peer(i)
        return copy_to(w_part.at[q], w_in.at[me], w1_s.at[q], w1_r.at[me], device)

    def w2_copy(i):
        q, device = z_peer(i)
        return copy_to(w_mid.at[z], w_mid.at[z], w2_s.at[q], w2_r.at[z], device)

    def w3_copy(i):
        q, device = plane_peer(i)
        return copy_to(w_all.at[me], w_all.at[me], w3_s.at[q], w3_r.at[me], device)

    for i in range(1, n_plane):
        w1_copy(i).start()
    backward(r)
    w_in[me] = w_part[me]
    for i in range(1, n_plane):
        arrive(w_in, w1_r, (me + i) % n_plane)
    w_mid[z] = jnp.sum(w_in[...].astype(F32), axis=0).astype(BF16)
    for i in range(1, n_z):
        w2_copy(i).start()

    for i in range(1, n_z):
        arrive(w_mid, w2_r, (z + i) % n_z)
    w_all[me] = jnp.sum(w_mid[...].astype(F32), axis=0).astype(BF16)
    for i in range(1, n_plane):
        w3_copy(i).start()

    loads[6].wait()
    total = back[r].astype(F32)
    for i in range(1, n_row):
        q = (r + i) % n_row
        arrive(back_in, back_r, q)
        total += back_in[q].astype(F32)
    ordered = dot(order, total.astype(BF16)).astype(BF16)
    igrad_ref[...] = dot(ordered, weight_ref[...], ((1,), (1,))).astype(BF16)

    total = paired(z)
    for k in range(2):
        arrive(arrived, sum_r, k)
        total += arrived[k].astype(F32)
    out_ref[...] = dot((total / deg_row).astype(BF16), weight_ref[...], ((0,), (0,))).astype(BF16)

    for i in range(1, n_plane):
        arrive(w_all, w3_r, (me + i) % n_plane)
    for d in range(n_plane):
        wgrad_ref[d * slab : (d + 1) * slab, :] = w_all[d].astype(F32)

    for i in range(1, n_row):
        feat_copy(i)[1].wait_send()
        back_copy((r + i) % n_row).wait_send()
    for i in (1, 2, 3):
        grad_copy(i).wait_send()
    sum_copy(1).wait_send()

    @pl.when(inner)
    def _():
        for i in (2, 3):
            sum_copy(i).wait_send()

    @pl.when(end)
    def _():
        for i in (2, 3):
            pass_copy(i).wait_send()

    for i in range(n_z):
        zz = (z + i) % n_z
        relay_copy(zz * 2 + core).wait_send()
        pair_copy(zz).wait_send()

    for i in range(1, n_plane):
        w1_copy(i).wait_send()
        w3_copy(i).wait_send()
    for i in range(1, n_z):
        w2_copy(i).wait_send()


def layer(rows, cols, count, bits, features, cotangent, degrees, weight, n_row, n_z):
    n, width = features.shape
    n_col = 2 * n_z
    n_plane = 2 * n_row
    slots = bits.shape[0]
    block = lambda k: pltpu.VMEM((k, n, width), BF16)
    sems = lambda k: pltpu.SemaphoreType.DMA((k,))
    slab = lambda k: pltpu.VMEM((k, width // n_plane, width), BF16)
    tile = jax.ShapeDtypeStruct((n, width), BF16)
    return pl.pallas_call(
        functools.partial(layer_kernel, n_row, n_z),
        out_shape=(tile, jax.ShapeDtypeStruct((width, width), F32), tile),
        in_specs=[pl.BlockSpec(memory_space=VMEM)] + [pl.BlockSpec(memory_space=pltpu.HBM)] * 7,
        out_specs=(pl.BlockSpec(memory_space=VMEM),) * 3,
        scratch_shapes=[
            pltpu.VMEM((n * n_row, n * n_col), BF16),
            pltpu.VMEM((slots + 1, 8, 8, 128), jnp.int32),
            pltpu.VMEM((2, slots), jnp.int32),
            pltpu.SMEM((2, slots), jnp.int32),
            pltpu.VMEM((1, slots), jnp.int32),
            pltpu.VMEM((1, slots), jnp.int32),
            pltpu.VMEM((1, n), jnp.int32),
            pltpu.VMEM(bits.shape, jnp.int32),
            pltpu.VMEM((n, width), BF16),
            pltpu.VMEM((n, width), BF16),
            pltpu.VMEM((width, width), BF16),
            sems(7), pltpu.SemaphoreType.DMA,
            block(n_row), block(n_col), block(n_col), block(n_z), block(n_z), block(n_z), block(2),
            block(n_row), block(n_row), slab(n_plane), slab(n_plane), slab(n_z), slab(n_plane),
            sems(n_row), sems(n_row), sems(n_z), sems(n_col), sems(n_z), sems(n_z), sems(n_z),
            sems(n_z), sems(2), sems(n_z), sems(n_row), sems(n_row),
            sems(n_plane), sems(n_plane), sems(n_z), sems(n_z), sems(n_plane), sems(n_plane),
        ],
        compiler_params=pltpu.CompilerParams(
            collective_id=0, has_side_effects=True, vmem_limit_bytes=48 * 2**20
        ),
        name="layer",
    )(count, rows, cols, degrees, bits, features, cotangent, weight)


def swap_order(x, a, b):
    return x.reshape(-1, a, b, x.shape[-1]).swapaxes(1, 2).reshape(x.shape)


def per_device(features, cotangent, degrees, weight, tile_rows, tile_cols, tile_bits, tile_count):
    nodes, width = features.shape
    trows = nodes * lax.axis_size("col") // 128
    tcols = nodes * lax.axis_size("row") // 128
    n_row, n_col = lax.axis_size("row"), lax.axis_size("col")
    slots = tile_bits.shape[2]
    if n_row == 4 and n_col == 8 and nodes == width and trows * tcols < slots:
        return layer(
            tile_rows[0], tile_cols[0], tile_count, tile_bits[0, 0],
            features, cotangent, degrees.reshape(1, nodes), weight, n_row, n_col // 2,
        )
    at = build_adjacency(
        tile_count[0], tile_rows[0, 0], tile_cols[0, 0], tile_bits[0, 0], trows, tcols
    )
    deg = degrees[:, None].astype(F32)
    scaled = (cotangent.astype(F32) / deg).astype(BF16)
    feats = lax.all_gather(swap_order(features, 16, 8), "row", axis=0, tiled=True)
    grads = lax.all_gather(scaled, "col", axis=0, tiled=True)
    fwd = lax.dot_general(at, feats, (((0,), (0,)), ((), ())), preferred_element_type=F32)
    fwd = fwd.astype(BF16)
    local = lax.dot_general(fwd, grads, (((0,), (0,)), ((), ())), preferred_element_type=F32)
    weight_grad = lax.psum(local, ("row", "col"))
    summed = lax.psum_scatter(fwd, "col", scatter_dimension=0, tiled=True).astype(F32)
    aggregated = (summed / deg).astype(BF16)
    output = jnp.dot(aggregated, weight, preferred_element_type=F32).astype(BF16)
    bwd = jnp.dot(at, grads, preferred_element_type=F32).astype(BF16)
    back = swap_order(lax.psum_scatter(bwd, "row", scatter_dimension=0, tiled=True), 8, 16)
    input_grad = jnp.dot(back, weight.T, preferred_element_type=F32).astype(BF16)
    return output, weight_grad, input_grad


def solution(mesh):
    placed = (
        P(("col", "row"), None),
        P(("row", "col"), None),
        P(("row", "col")),
        P(),
        P("row", "col", None),
        P("row", "col", None),
        P("row", "col", None, None, None),
        P("row", "col"),
    )
    return jax.shard_map(
        per_device,
        mesh=mesh,
        in_specs=placed,
        out_specs=(P(("row", "col"), None), P(), P(("col", "row"), None)),
        check_vma=False,
    )
```

```python
import functools

import jax
import jax.numpy as jnp
from jax import lax
from jax.experimental import pallas as pl
from jax.experimental.pallas import tpu as pltpu
from jax.sharding import PartitionSpec as P

SMEM = pltpu.SMEM
VMEM = pltpu.VMEM
BF16 = jnp.bfloat16
F32 = jnp.float32


def build_kernel(trows, chunk, count_ref, rows_ref, cols_ref, bits_ref, out_ref, acc0, acc1):
    base = pl.program_id(0) * chunk
    zero = jnp.zeros(acc0.shape[1:], jnp.int32)

    def clear(p, carry):
        acc0[p] = zero
        acc1[p] = zero
        return carry

    lax.fori_loop(0, chunk * trows, clear, 0, unroll=4)
    count = count_ref[0]

    def add_pair(k, carry):
        for half, acc in enumerate((acc0, acc1)):
            s = 2 * k + half
            col = cols_ref[s] - base
            ok = (s < count) & (col >= 0) & (col < chunk)
            p = jnp.where(ok, col * trows + rows_ref[s], 0)
            words = bits_ref[s]
            word = (words[:8] | (words[8:] << 16)) & (0 - ok.astype(jnp.int32))
            for b in range(8):
                acc[p, b] += (word >> b) & 0x10001
        return carry

    lax.fori_loop(0, (count + 1) // 2, add_pair, 0)

    def convert(row, carry):
        lanes = pl.ds(pl.multiple_of(row * 128, 128), 128)
        for col in range(chunk):
            p = col * trows + row
            for b in range(8):
                v = acc0[p, b] + acc1[p, b]
                both = jnp.concatenate([v & 0xFFFF, v >> 16], axis=0)
                out_ref[pl.ds(col * 128 + b * 16, 16), lanes] = both.astype(F32).astype(BF16)
        return carry

    lax.fori_loop(0, trows, convert, 0)


def build_adjacency(count, rows, cols, bits, trows, tcols):
    chunk = max(d for d in range(1, tcols + 1) if tcols % d == 0 and d * trows <= 128)
    scratch = pltpu.VMEM((chunk * trows, 8, 8, 128), jnp.int32)
    return pl.pallas_call(
        functools.partial(build_kernel, trows, chunk),
        grid=(tcols // chunk,),
        out_shape=jax.ShapeDtypeStruct((tcols * 128, trows * 128), BF16),
        in_specs=[
            pl.BlockSpec(memory_space=SMEM),
            pl.BlockSpec(memory_space=SMEM),
            pl.BlockSpec(memory_space=SMEM),
            pl.BlockSpec(memory_space=VMEM),
        ],
        out_specs=pl.BlockSpec((chunk * 128, trows * 128), lambda g: (g, 0)),
        scratch_shapes=[scratch, scratch],
        compiler_params=pltpu.CompilerParams(vmem_limit_bytes=40 * 2**20),
        name="build_adjacency",
    )(count, rows, cols, bits)


MESH = pl.DeviceIdType.MESH


def copy_to(src, dst, send_sem, recv_sem, device):
    return pltpu.make_async_remote_copy(
        src_ref=src,
        dst_ref=dst,
        send_sem=send_sem,
        recv_sem=recv_sem,
        device_id=device,
        device_id_type=MESH,
    )


def dot(a, b, dims=((1,), (0,))):
    return lax.dot_general(a, b, (dims, ((), ())), preferred_element_type=F32)


def layer_kernel(
    n_row, n_z,
    count_ref, rows_hbm, cols_hbm, deg_hbm, bits_hbm, feat_hbm, cot_hbm, weight_hbm,
    out_ref, wgrad_ref, igrad_ref,
    at_ref, prefix, plan, plan_smem, rows_ref, cols_ref, deg_ref, bits_ref, feat_ref, cot_ref, weight_ref, load_s, plan_s,
    feats, grads, part, pair, sums, passed, arrived, back, back_sum, back_in, w_part, w_in, w_mid, w_all,
    feat_s, feat_r, grad_s, grad_r, relay_s, pair_s, pair_r, sum_s, sum_r, pass_r, back_s, back_r,
    w1_s, w1_r, w2_s, w2_r, w3_s, w3_r,
):
    n = feat_ref.shape[0]
    n_col = 2 * n_z
    n_plane = n_row * 2
    r = lax.axis_index("row")
    c = lax.axis_index("col")
    z = c // 2
    core = c % 2
    sibling = (r, z * 2 + 1 - core)

    me = r * 2 + core

    def plane_peer(i):
        q = (me + i) % n_plane
        return q, (q // 2, z * 2 + q % 2)

    def z_peer(i):
        zz = (z + i) % n_z
        return zz, (r, zz * 2 + core)

    def flip(i):
        return ((z // 2 + i // 2) % 2) * 2 + (z + i) % 2

    mate = flip(1)
    inner = z % 2 != z // 2
    end = z % 2 == z // 2

    def at_z(zz):
        return (r, zz * 2 + core)

    barrier = pltpu.get_barrier_semaphore()
    for i in range(1, n_plane):
        pl.semaphore_signal(barrier, inc=1, device_id=plane_peer(i)[1], device_id_type=MESH)
    for i in range(1, n_z):
        pl.semaphore_signal(barrier, inc=1, device_id=z_peer(i)[1], device_id_type=MESH)
    loads = [
        pltpu.make_async_copy(src, dst, load_s.at[k])
        for k, (src, dst) in enumerate(
            (
                (rows_hbm, rows_ref), (cols_hbm, cols_ref), (deg_hbm, deg_ref), (cot_hbm, cot_ref),
                (feat_hbm, feat_ref), (bits_hbm, bits_ref), (weight_hbm, weight_ref),
            )
        )
    ]
    for load in loads:
        load.start()

    i0 = lax.broadcasted_iota(jnp.int32, (n, n), 0)
    i1 = lax.broadcasted_iota(jnp.int32, (n, n), 1)
    placed = (i1 // 128) * 128 + (i1 % 16) * 8 + (i1 % 128) // 16
    order = (i0 == placed).astype(F32).astype(BF16)
    loads[2].wait()
    deg_row = deg_ref[...].astype(F32)
    deg_col = jnp.sum(jnp.where(i0 == i1, deg_row, 0.0), axis=1, keepdims=True)
    loads[3].wait()
    grads[c] = (cot_ref[...].astype(F32) / deg_col).astype(BF16)

    pl.semaphore_wait(barrier, n_plane + n_z - 2)

    def feat_copy(i):
        q = (r + i) % n_row
        return q, copy_to(feats.at[r], feats.at[r], feat_s.at[q], feat_r.at[r], (q, c))

    def grad_copy(i):
        return copy_to(grads.at[c], grads.at[c], grad_s.at[i], grad_r.at[c], at_z(flip(i)))

    def relay_copy(q):
        return copy_to(grads.at[q], grads.at[q], relay_s.at[q // 2], grad_r.at[q], sibling)

    for i in (3, 2, 1):
        grad_copy(i).start()
    relay_copy(c).start()
    loads[4].wait()
    feats[r] = dot(feat_ref[...], order, ((0,), (0,))).astype(BF16)
    for i in range(1, n_row):
        feat_copy(i)[1].start()

    loads[0].wait()
    loads[1].wait()
    trows = n * n_col // 128
    tcols = n * n_row // 128
    places = trows * tcols
    slots = rows_ref.shape[1]
    s0 = lax.broadcasted_iota(jnp.int32, (slots, slots), 0)
    s1 = lax.broadcasted_iota(jnp.int32, (slots, slots), 1)
    lane = lax.broadcasted_iota(jnp.int32, (1, slots), 1)
    place = jnp.where(lane < count_ref[...], cols_ref[...] * trows + rows_ref[...], places)
    key_row = (place * slots + lane).astype(F32)
    key_col = jnp.sum(jnp.where(s0 == s1, key_row, 0.0), axis=1, keepdims=True)
    rank = jnp.sum((key_row < key_col).astype(F32), axis=1, keepdims=True)
    picked = jnp.where(rank == s1.astype(F32), s0, 0)
    before = (key_col < (s1 * slots).astype(F32)).astype(jnp.int32)
    plan[0:1, :] = jnp.clip(jnp.sum(picked, axis=0, keepdims=True), 0, slots - 1)
    plan[1:2, :] = jnp.clip(jnp.sum(before, axis=0, keepdims=True), 0, slots)
    plan_copy = pltpu.make_async_copy(plan, plan_smem, plan_s)
    plan_copy.start()


    def arrive(ref, sem, slot):
        copy_to(ref.at[slot], ref.at[slot], sem.at[slot], sem.at[slot], sibling).wait_recv()

    plan_copy.wait()
    loads[5].wait()
    zero = jnp.zeros((8, 128), jnp.int32)
    for b in range(8):
        prefix[0, b] = zero

    def add_slot(k, totals):
        words = bits_ref[plan_smem[0, k]]
        word = words[:8] | (words[8:] << 16)
        totals = tuple(t + ((word >> b) & 0x10001) for b, t in enumerate(totals))
        for b in range(8):
            prefix[k + 1, b] = totals[b]
        return totals

    lax.fori_loop(0, slots, add_slot, (zero,) * 8, unroll=4)

    def place_row(row, carry):
        lanes = pl.ds(pl.multiple_of(row * 128, 128), 128)
        for col in range(tcols):
            p = col * trows + row
            first = plan_smem[1, p]
            last = plan_smem[1, p + 1]
            for b in range(8):
                v = prefix[last, b] - prefix[first, b]
                both = jnp.concatenate([v & 0xFFFF, v >> 16], axis=0)
                at_ref[pl.ds(col * 128 + b * 16, 16), lanes] = both.astype(F32).astype(BF16)
        return carry

    lax.fori_loop(0, trows, place_row, 0)

    for i in range(1, n_row):
        arrive(feats, feat_r, (r + i) % n_row)

    def forward(q):
        lanes = pl.ds(pl.multiple_of(q * n, n), n)
        total = dot(feats[0], at_ref[pl.ds(0, n), lanes])
        for k in range(1, n_row):
            total += dot(feats[k], at_ref[pl.ds(k * n, n), lanes])
        part[q] = total.astype(BF16)

    def pair_copy(zz):
        q = zz * 2 + 1 - core
        return copy_to(part.at[q], pair.at[zz], pair_s.at[zz], pair_r.at[zz], sibling)

    @pl.loop(0, n_z)
    def _(i):
        zz = flip(3 - i)
        forward(zz * 2 + 1 - core)
        pair_copy(zz).start()

    @pl.loop(0, n_z)
    def _(i):
        forward(flip(3 - i) * 2 + core)

    def paired(zz):
        arrive(pair, pair_r, zz)
        return part[zz * 2 + core].astype(F32) + pair[zz].astype(F32)

    def pass_copy(i):
        zz = flip(i)
        return copy_to(sums.at[zz], passed.at[zz], sum_s.at[zz], pass_r.at[zz], at_z(mate))

    def sum_copy(i):
        zz = flip(i)
        k = 0 if i == 1 else 1
        return copy_to(sums.at[zz], arrived.at[k], sum_s.at[zz], sum_r.at[k], at_z(zz))

    @pl.when(end)
    def _():
        for i in (3, 2):
            sums[flip(i)] = paired(flip(i)).astype(BF16)
            pass_copy(i).start()

    sums[mate] = paired(mate).astype(BF16)
    sum_copy(1).start()

    def add_back(q):
        lanes = pl.ds(pl.multiple_of(q * n, n), n)
        return dot(at_ref[:, lanes], grads[q])

    back_sum[...] = add_back(c)
    for i in (1, 2, 3):
        q = flip(i) * 2 + core
        arrive(grads, grad_r, q)
        relay_copy(q).start()
        back_sum[...] += add_back(q)
    for i in range(n_z):
        q = flip(i) * 2 + 1 - core
        arrive(grads, grad_r, q)
        back_sum[...] += add_back(q)

    def back_copy(q):
        return copy_to(back.at[q], back_in.at[r], back_s.at[q], back_r.at[r], (q, c))

    for i in range(1, n_row):
        q = (r + i) % n_row
        back[q] = back_sum[pl.ds(pl.multiple_of(q * n, n), n), :].astype(BF16)
        back_copy(q).start()

    @pl.when(inner)
    def _():
        for i in (2, 3):
            zz = flip(i)
            total = paired(zz)
            arrive(passed, pass_r, zz)
            sums[zz] = (total + passed[zz].astype(F32)).astype(BF16)
            sum_copy(i).start()

    local = dot(part[0], grads[0])
    for q in range(1, n_col):
        local += dot(part[q], grads[q])
    rounded = local.astype(BF16)
    slab = rounded.shape[0] // n_plane
    for d in range(n_plane):
        w_part[d] = rounded[d * slab : (d + 1) * slab]

    def w1_copy(i):
        q, device = plane_peer(i)
        return copy_to(w_part.at[q], w_in.at[me], w1_s.at[q], w1_r.at[me], device)

    def w2_copy(i):
        q, device = z_peer(i)
        return copy_to(w_mid.at[z], w_mid.at[z], w2_s.at[q], w2_r.at[z], device)

    def w3_copy(i):
        q, device = plane_peer(i)
        return copy_to(w_all.at[me], w_all.at[me], w3_s.at[q], w3_r.at[me], device)

    for i in range(1, n_plane):
        w1_copy(i).start()
    w_in[me] = w_part[me]
    for i in range(1, n_plane):
        arrive(w_in, w1_r, (me + i) % n_plane)
    w_mid[z] = jnp.sum(w_in[...].astype(F32), axis=0).astype(BF16)
    for i in range(1, n_z):
        w2_copy(i).start()

    for i in range(1, n_z):
        arrive(w_mid, w2_r, (z + i) % n_z)
    w_all[me] = jnp.sum(w_mid[...].astype(F32), axis=0).astype(BF16)
    for i in range(1, n_plane):
        w3_copy(i).start()

    loads[6].wait()
    total = back_sum[pl.ds(pl.multiple_of(r * n, n), n), :]
    for i in range(1, n_row):
        q = (r + i) % n_row
        arrive(back_in, back_r, q)
        total += back_in[q].astype(F32)
    ordered = dot(order, total.astype(BF16)).astype(BF16)
    igrad_ref[...] = dot(ordered, weight_ref[...], ((1,), (1,))).astype(BF16)

    total = paired(z)
    for k in range(2):
        arrive(arrived, sum_r, k)
        total += arrived[k].astype(F32)
    out_ref[...] = dot((total / deg_row).astype(BF16), weight_ref[...], ((0,), (0,))).astype(BF16)

    for i in range(1, n_plane):
        arrive(w_all, w3_r, (me + i) % n_plane)
    for d in range(n_plane):
        wgrad_ref[d * slab : (d + 1) * slab, :] = w_all[d].astype(F32)

    for i in range(1, n_row):
        feat_copy(i)[1].wait_send()
        back_copy((r + i) % n_row).wait_send()
    for i in (1, 2, 3):
        grad_copy(i).wait_send()
    sum_copy(1).wait_send()

    @pl.when(inner)
    def _():
        for i in (2, 3):
            sum_copy(i).wait_send()

    @pl.when(end)
    def _():
        for i in (2, 3):
            pass_copy(i).wait_send()

    for i in range(n_z):
        zz = (z + i) % n_z
        relay_copy(zz * 2 + core).wait_send()
        pair_copy(zz).wait_send()

    for i in range(1, n_plane):
        w1_copy(i).wait_send()
        w3_copy(i).wait_send()
    for i in range(1, n_z):
        w2_copy(i).wait_send()


def place_kernel(*refs):
    n = len(refs) // 2
    copies = [pltpu.make_async_copy(refs[k], refs[n + k], refs[-1].at[k]) for k in range(n)]
    for copy in copies:
        copy.start()
    for copy in copies:
        copy.wait()


def place(arrays):
    return pl.pallas_call(
        place_kernel,
        out_shape=tuple(jax.ShapeDtypeStruct(x.shape, x.dtype) for x in arrays),
        in_specs=[pl.BlockSpec(memory_space=pl.ANY)] * len(arrays),
        out_specs=(pl.BlockSpec(memory_space=pl.ANY),) * len(arrays),
        scratch_shapes=[pltpu.SemaphoreType.DMA((len(arrays),))],
        compiler_params=pltpu.CompilerParams(vmem_limit_bytes=64 * 2**20),
        name="place",
    )(*arrays)


def layer(rows, cols, count, bits, features, cotangent, degrees, weight, n_row, n_z):
    n, width = features.shape
    n_col = 2 * n_z
    n_plane = 2 * n_row
    slots = bits.shape[0]
    block = lambda k: pltpu.VMEM((k, n, width), BF16)
    sems = lambda k: pltpu.SemaphoreType.DMA((k,))
    slab = lambda k: pltpu.VMEM((k, width // n_plane, width), BF16)
    tile = jax.ShapeDtypeStruct((n, width), BF16)
    return pl.pallas_call(
        functools.partial(layer_kernel, n_row, n_z),
        out_shape=(tile, jax.ShapeDtypeStruct((width, width), F32), tile),
        in_specs=[pl.BlockSpec(memory_space=VMEM)] + [pl.BlockSpec(memory_space=pltpu.HBM)] * 7,
        out_specs=(pl.BlockSpec(memory_space=VMEM),) * 3,
        scratch_shapes=[
            pltpu.VMEM((n * n_row, n * n_col), BF16),
            pltpu.VMEM((slots + 1, 8, 8, 128), jnp.int32),
            pltpu.VMEM((2, slots), jnp.int32),
            pltpu.SMEM((2, slots), jnp.int32),
            pltpu.VMEM((1, slots), jnp.int32),
            pltpu.VMEM((1, slots), jnp.int32),
            pltpu.VMEM((1, n), jnp.int32),
            pltpu.VMEM(bits.shape, jnp.int32),
            pltpu.VMEM((n, width), BF16),
            pltpu.VMEM((n, width), BF16),
            pltpu.VMEM((width, width), BF16),
            sems(7), pltpu.SemaphoreType.DMA,
            block(n_row), block(n_col), block(n_col), block(n_z), block(n_z), block(n_z), block(2),
            block(n_row), pltpu.VMEM((n * n_row, width), F32), block(n_row), slab(n_plane), slab(n_plane), slab(n_z), slab(n_plane),
            sems(n_row), sems(n_row), sems(n_z), sems(n_col), sems(n_z), sems(n_z), sems(n_z),
            sems(n_z), sems(2), sems(n_z), sems(n_row), sems(n_row),
            sems(n_plane), sems(n_plane), sems(n_z), sems(n_z), sems(n_plane), sems(n_plane),
        ],
        compiler_params=pltpu.CompilerParams(
            collective_id=0, has_side_effects=True, vmem_limit_bytes=64 * 2**20
        ),
        name="layer",
    )(count, rows, cols, degrees, bits, features, cotangent, weight)


def swap_order(x, a, b):
    return x.reshape(-1, a, b, x.shape[-1]).swapaxes(1, 2).reshape(x.shape)


def per_device(features, cotangent, degrees, weight, tile_rows, tile_cols, tile_bits, tile_count):
    nodes, width = features.shape
    trows = nodes * lax.axis_size("col") // 128
    tcols = nodes * lax.axis_size("row") // 128
    n_row, n_col = lax.axis_size("row"), lax.axis_size("col")
    slots = tile_bits.shape[2]
    if n_row == 4 and n_col == 8 and nodes == width and trows * tcols < slots:
        results = layer(
            tile_rows[0], tile_cols[0], tile_count, tile_bits[0, 0],
            features, cotangent, degrees.reshape(1, nodes), weight, n_row, n_col // 2,
        )
        return place(results)
    at = build_adjacency(
        tile_count[0], tile_rows[0, 0], tile_cols[0, 0], tile_bits[0, 0], trows, tcols
    )
    deg = degrees[:, None].astype(F32)
    scaled = (cotangent.astype(F32) / deg).astype(BF16)
    feats = lax.all_gather(swap_order(features, 16, 8), "row", axis=0, tiled=True)
    grads = lax.all_gather(scaled, "col", axis=0, tiled=True)
    fwd = lax.dot_general(at, feats, (((0,), (0,)), ((), ())), preferred_element_type=F32)
    fwd = fwd.astype(BF16)
    local = lax.dot_general(fwd, grads, (((0,), (0,)), ((), ())), preferred_element_type=F32)
    weight_grad = lax.psum(local, ("row", "col"))
    summed = lax.psum_scatter(fwd, "col", scatter_dimension=0, tiled=True).astype(F32)
    aggregated = (summed / deg).astype(BF16)
    output = jnp.dot(aggregated, weight, preferred_element_type=F32).astype(BF16)
    bwd = jnp.dot(at, grads, preferred_element_type=F32).astype(BF16)
    back = swap_order(lax.psum_scatter(bwd, "row", scatter_dimension=0, tiled=True), 8, 16)
    input_grad = jnp.dot(back, weight.T, preferred_element_type=F32).astype(BF16)
    return output, weight_grad, input_grad


def solution(mesh):
    placed = (
        P(("col", "row"), None),
        P(("row", "col"), None),
        P(("row", "col")),
        P(),
        P("row", "col", None),
        P("row", "col", None),
        P("row", "col", None, None, None),
        P("row", "col"),
    )
    return jax.shard_map(
        per_device,
        mesh=mesh,
        in_specs=placed,
        out_specs=(P(("row", "col"), None), P(), P(("col", "row"), None)),
        check_vma=False,
    )
```

```python
import functools

import jax
import jax.numpy as jnp
from jax import lax
from jax.experimental import pallas as pl
from jax.experimental.pallas import tpu as pltpu
from jax.sharding import PartitionSpec as P

SMEM = pltpu.SMEM
VMEM = pltpu.VMEM
BF16 = jnp.bfloat16
F32 = jnp.float32


def build_kernel(trows, chunk, count_ref, rows_ref, cols_ref, bits_ref, out_ref, acc0, acc1):
    base = pl.program_id(0) * chunk
    zero = jnp.zeros(acc0.shape[1:], jnp.int32)

    def clear(p, carry):
        acc0[p] = zero
        acc1[p] = zero
        return carry

    lax.fori_loop(0, chunk * trows, clear, 0, unroll=4)
    count = count_ref[0]

    def add_pair(k, carry):
        for half, acc in enumerate((acc0, acc1)):
            s = 2 * k + half
            col = cols_ref[s] - base
            ok = (s < count) & (col >= 0) & (col < chunk)
            p = jnp.where(ok, col * trows + rows_ref[s], 0)
            words = bits_ref[s]
            word = (words[:8] | (words[8:] << 16)) & (0 - ok.astype(jnp.int32))
            for b in range(8):
                acc[p, b] += (word >> b) & 0x10001
        return carry

    lax.fori_loop(0, (count + 1) // 2, add_pair, 0)

    def convert(row, carry):
        lanes = pl.ds(pl.multiple_of(row * 128, 128), 128)
        for col in range(chunk):
            p = col * trows + row
            for b in range(8):
                v = acc0[p, b] + acc1[p, b]
                both = jnp.concatenate([v & 0xFFFF, v >> 16], axis=0)
                out_ref[pl.ds(col * 128 + b * 16, 16), lanes] = both.astype(F32).astype(BF16)
        return carry

    lax.fori_loop(0, trows, convert, 0)


def build_adjacency(count, rows, cols, bits, trows, tcols):
    chunk = max(d for d in range(1, tcols + 1) if tcols % d == 0 and d * trows <= 128)
    scratch = pltpu.VMEM((chunk * trows, 8, 8, 128), jnp.int32)
    return pl.pallas_call(
        functools.partial(build_kernel, trows, chunk),
        grid=(tcols // chunk,),
        out_shape=jax.ShapeDtypeStruct((tcols * 128, trows * 128), BF16),
        in_specs=[
            pl.BlockSpec(memory_space=SMEM),
            pl.BlockSpec(memory_space=SMEM),
            pl.BlockSpec(memory_space=SMEM),
            pl.BlockSpec(memory_space=VMEM),
        ],
        out_specs=pl.BlockSpec((chunk * 128, trows * 128), lambda g: (g, 0)),
        scratch_shapes=[scratch, scratch],
        compiler_params=pltpu.CompilerParams(vmem_limit_bytes=40 * 2**20),
        name="build_adjacency",
    )(count, rows, cols, bits)


MESH = pl.DeviceIdType.MESH


def copy_to(src, dst, send_sem, recv_sem, device):
    return pltpu.make_async_remote_copy(
        src_ref=src,
        dst_ref=dst,
        send_sem=send_sem,
        recv_sem=recv_sem,
        device_id=device,
        device_id_type=MESH,
    )


def dot(a, b, dims=((1,), (0,))):
    return lax.dot_general(a, b, (dims, ((), ())), preferred_element_type=F32)


def layer_kernel(
    n_row, n_z,
    count_ref, rows_hbm, cols_hbm, deg_hbm, bits_hbm, feat_hbm, cot_hbm, weight_hbm,
    out_ref, wgrad_ref, igrad_ref,
    at_ref, prefix, plan, plan_smem, rows_ref, cols_ref, deg_ref, bits_ref, feat_ref, cot_ref, weight_ref, load_s, plan_s,
    feats, grads, part, pair, sums, passed, arrived, back, back_sum, back_in, w_part, w_in, w_mid, w_all,
    feat_s, feat_r, grad_s, grad_r, relay_s, pair_s, pair_r, sum_s, sum_r, pass_r, back_s, back_r,
    w1_s, w1_r, w2_s, w2_r, w3_s, w3_r,
):
    n = feat_ref.shape[0]
    n_col = 2 * n_z
    n_plane = n_row * 2
    r = lax.axis_index("row")
    c = lax.axis_index("col")
    z = c // 2
    core = c % 2
    sibling = (r, z * 2 + 1 - core)

    me = r * 2 + core

    def plane_peer(i):
        q = (me + i) % n_plane
        return q, (q // 2, z * 2 + q % 2)

    def z_peer(i):
        zz = (z + i) % n_z
        return zz, (r, zz * 2 + core)

    def flip(i):
        return ((z // 2 + i // 2) % 2) * 2 + (z + i) % 2

    mate = flip(1)
    inner = z % 2 != z // 2
    end = z % 2 == z // 2

    def at_z(zz):
        return (r, zz * 2 + core)

    barrier = pltpu.get_barrier_semaphore()
    for i in range(1, n_plane):
        pl.semaphore_signal(barrier, inc=1, device_id=plane_peer(i)[1], device_id_type=MESH)
    for i in range(1, n_z):
        pl.semaphore_signal(barrier, inc=1, device_id=z_peer(i)[1], device_id_type=MESH)
    loads = [
        pltpu.make_async_copy(src, dst, load_s.at[k])
        for k, (src, dst) in enumerate(
            (
                (rows_hbm, rows_ref), (cols_hbm, cols_ref), (deg_hbm, deg_ref), (cot_hbm, cot_ref),
                (feat_hbm, feat_ref), (bits_hbm, bits_ref), (weight_hbm, weight_ref),
            )
        )
    ]
    for load in loads:
        load.start()

    i0 = lax.broadcasted_iota(jnp.int32, (n, n), 0)
    i1 = lax.broadcasted_iota(jnp.int32, (n, n), 1)
    placed = (i1 // 128) * 128 + (i1 % 16) * 8 + (i1 % 128) // 16
    order = (i0 == placed).astype(F32).astype(BF16)
    loads[2].wait()
    deg_row = deg_ref[...].astype(F32)
    deg_col = jnp.sum(jnp.where(i0 == i1, deg_row, 0.0), axis=1, keepdims=True)
    loads[3].wait()
    grads[c] = (cot_ref[...].astype(F32) / deg_col).astype(BF16)

    loads[4].wait()
    feats[r] = dot(feat_ref[...], order, ((0,), (0,))).astype(BF16)
    pl.semaphore_wait(barrier, n_plane + n_z - 2)

    def feat_copy(i):
        q = (r + i) % n_row
        return q, copy_to(feats.at[r], feats.at[r], feat_s.at[q], feat_r.at[r], (q, c))

    def grad_copy(i):
        return copy_to(grads.at[c], grads.at[c], grad_s.at[i], grad_r.at[c], at_z(flip(i)))

    def relay_copy(q):
        return copy_to(grads.at[q], grads.at[q], relay_s.at[q // 2], grad_r.at[q], sibling)

    for i in range(1, n_row):
        feat_copy(i)[1].start()
    for i in (3, 2, 1):
        grad_copy(i).start()
    relay_copy(c).start()

    loads[0].wait()
    loads[1].wait()
    trows = n * n_col // 128
    tcols = n * n_row // 128
    places = trows * tcols
    slots = rows_ref.shape[1]
    s0 = lax.broadcasted_iota(jnp.int32, (slots, slots), 0)
    s1 = lax.broadcasted_iota(jnp.int32, (slots, slots), 1)
    lane = lax.broadcasted_iota(jnp.int32, (1, slots), 1)
    place = jnp.where(lane < count_ref[...], cols_ref[...] * trows + rows_ref[...], places)
    key_row = (place * slots + lane).astype(F32)
    key_col = jnp.sum(jnp.where(s0 == s1, key_row, 0.0), axis=1, keepdims=True)
    rank = jnp.sum((key_row < key_col).astype(F32), axis=1, keepdims=True)
    picked = jnp.where(rank == s1.astype(F32), s0, 0)
    before = (key_col < (s1 * slots).astype(F32)).astype(jnp.int32)
    plan[0:1, :] = jnp.clip(jnp.sum(picked, axis=0, keepdims=True), 0, slots - 1)
    plan[1:2, :] = jnp.clip(jnp.sum(before, axis=0, keepdims=True), 0, slots)
    plan_copy = pltpu.make_async_copy(plan, plan_smem, plan_s)
    plan_copy.start()


    def arrive(ref, sem, slot):
        copy_to(ref.at[slot], ref.at[slot], sem.at[slot], sem.at[slot], sibling).wait_recv()

    plan_copy.wait()
    loads[5].wait()
    zero = jnp.zeros((8, 128), jnp.int32)
    for b in range(8):
        prefix[0, b] = zero

    def add_slot(k, totals):
        words = bits_ref[plan_smem[0, k]]
        word = words[:8] | (words[8:] << 16)
        totals = tuple(t + ((word >> b) & 0x10001) for b, t in enumerate(totals))
        for b in range(8):
            prefix[k + 1, b] = totals[b]
        return totals

    lax.fori_loop(0, slots, add_slot, (zero,) * 8, unroll=4)

    def place_row(row, carry):
        lanes = pl.ds(pl.multiple_of(row * 128, 128), 128)
        for col in range(tcols):
            p = col * trows + row
            first = plan_smem[1, p]
            last = plan_smem[1, p + 1]
            for b in range(8):
                v = prefix[last, b] - prefix[first, b]
                both = jnp.concatenate([v & 0xFFFF, v >> 16], axis=0)
                at_ref[pl.ds(col * 128 + b * 16, 16), lanes] = both.astype(F32).astype(BF16)
        return carry

    lax.fori_loop(0, trows, place_row, 0)

    for i in range(1, n_row):
        arrive(feats, feat_r, (r + i) % n_row)

    def forward(q):
        lanes = pl.ds(pl.multiple_of(q * n, n), n)
        total = dot(feats[0], at_ref[pl.ds(0, n), lanes])
        for k in range(1, n_row):
            total += dot(feats[k], at_ref[pl.ds(k * n, n), lanes])
        part[q] = total.astype(BF16)

    def pair_copy(zz):
        q = zz * 2 + 1 - core
        return copy_to(part.at[q], pair.at[zz], pair_s.at[zz], pair_r.at[zz], sibling)

    @pl.loop(0, n_z)
    def _(i):
        zz = flip(3 - i)
        forward(zz * 2 + 1 - core)
        pair_copy(zz).start()

    @pl.loop(0, n_z)
    def _(i):
        forward(flip(3 - i) * 2 + core)

    def paired(zz):
        arrive(pair, pair_r, zz)
        return part[zz * 2 + core].astype(F32) + pair[zz].astype(F32)

    def pass_copy(i):
        zz = flip(i)
        return copy_to(sums.at[zz], passed.at[zz], sum_s.at[zz], pass_r.at[zz], at_z(mate))

    def sum_copy(i):
        zz = flip(i)
        k = 0 if i == 1 else 1
        return copy_to(sums.at[zz], arrived.at[k], sum_s.at[zz], sum_r.at[k], at_z(zz))

    @pl.when(end)
    def _():
        sums[flip(3)] = paired(flip(3)).astype(BF16)
        pass_copy(3).start()
        sums[flip(2)] = paired(flip(2)).astype(BF16)

    sums[mate] = paired(mate).astype(BF16)

    @pl.when(inner)
    def _():
        sum_copy(1).start()

    def add_back(q):
        lanes = pl.ds(pl.multiple_of(q * n, n), n)
        return dot(at_ref[:, lanes], grads[q])

    back_sum[...] = add_back(c)

    @pl.when(end)
    def _():
        pass_copy(3).wait_send()
        pass_copy(2).start()

    for i in (1, 2, 3):
        q = flip(i) * 2 + core
        arrive(grads, grad_r, q)
        relay_copy(q).start()
        back_sum[...] += add_back(q)

    @pl.when(end)
    def _():
        pass_copy(2).wait_send()
        sum_copy(1).start()

    for i in range(n_z):
        q = flip(i) * 2 + 1 - core
        arrive(grads, grad_r, q)
        back_sum[...] += add_back(q)

    def back_copy(q):
        return copy_to(back.at[q], back_in.at[r], back_s.at[q], back_r.at[r], (q, c))

    for i in range(1, n_row):
        q = (r + i) % n_row
        back[q] = back_sum[pl.ds(pl.multiple_of(q * n, n), n), :].astype(BF16)
        back_copy(q).start()

    def add_passed(i):
        zz = flip(i)
        total = paired(zz)
        arrive(passed, pass_r, zz)
        sums[zz] = (total + passed[zz].astype(F32)).astype(BF16)
        sum_copy(i).start()

    @pl.when(inner)
    def _():
        add_passed(2)

    local = dot(part[0], grads[0])
    for q in range(1, n_col):
        local += dot(part[q], grads[q])
    rounded = local.astype(BF16)
    slab = rounded.shape[0] // n_plane
    for d in range(n_plane):
        w_part[d] = rounded[d * slab : (d + 1) * slab]

    def w1_copy(i):
        q, device = plane_peer(i)
        return copy_to(w_part.at[q], w_in.at[me], w1_s.at[q], w1_r.at[me], device)

    def w2_copy(i):
        q, device = z_peer(i)
        return copy_to(w_mid.at[z], w_mid.at[z], w2_s.at[q], w2_r.at[z], device)

    def w3_copy(i):
        q, device = plane_peer(i)
        return copy_to(w_all.at[me], w_all.at[me], w3_s.at[q], w3_r.at[me], device)

    for i in range(1, n_plane):
        w1_copy(i).start()

    @pl.when(inner)
    def _():
        add_passed(3)

    w_in[me] = w_part[me]
    for i in range(1, n_plane):
        arrive(w_in, w1_r, (me + i) % n_plane)
    w_mid[z] = jnp.sum(w_in[...].astype(F32), axis=0).astype(BF16)
    for i in range(1, n_z):
        w2_copy(i).start()

    for i in range(1, n_z):
        arrive(w_mid, w2_r, (z + i) % n_z)
    w_all[me] = jnp.sum(w_mid[...].astype(F32), axis=0).astype(BF16)
    for i in range(1, n_plane):
        w3_copy(i).start()

    loads[6].wait()
    total = back_sum[pl.ds(pl.multiple_of(r * n, n), n), :]
    for i in range(1, n_row):
        q = (r + i) % n_row
        arrive(back_in, back_r, q)
        total += back_in[q].astype(F32)
    ordered = dot(order, total.astype(BF16)).astype(BF16)
    igrad_ref[...] = dot(ordered, weight_ref[...], ((1,), (1,))).astype(BF16)

    total = paired(z)
    for k in range(2):
        arrive(arrived, sum_r, k)
        total += arrived[k].astype(F32)
    out_ref[...] = dot((total / deg_row).astype(BF16), weight_ref[...], ((0,), (0,))).astype(BF16)

    for i in range(1, n_plane):
        arrive(w_all, w3_r, (me + i) % n_plane)
    for d in range(n_plane):
        wgrad_ref[d * slab : (d + 1) * slab, :] = w_all[d].astype(F32)

    for i in range(1, n_row):
        feat_copy(i)[1].wait_send()
        back_copy((r + i) % n_row).wait_send()
    for i in (1, 2, 3):
        grad_copy(i).wait_send()
    sum_copy(1).wait_send()

    @pl.when(inner)
    def _():
        for i in (2, 3):
            sum_copy(i).wait_send()

    for i in range(n_z):
        zz = (z + i) % n_z
        relay_copy(zz * 2 + core).wait_send()
        pair_copy(zz).wait_send()

    for i in range(1, n_plane):
        w1_copy(i).wait_send()
        w3_copy(i).wait_send()
    for i in range(1, n_z):
        w2_copy(i).wait_send()


def place_kernel(*refs):
    n = len(refs) // 2
    for k in range(n):
        refs[n + k][...] = refs[k][...]


def place(arrays):
    return pl.pallas_call(
        place_kernel,
        out_shape=tuple(jax.ShapeDtypeStruct(x.shape, x.dtype) for x in arrays),
        in_specs=[pl.BlockSpec(memory_space=VMEM)] * len(arrays),
        out_specs=(pl.BlockSpec(memory_space=VMEM),) * len(arrays),
        compiler_params=pltpu.CompilerParams(vmem_limit_bytes=64 * 2**20),
        name="place",
    )(*arrays)


def layer(rows, cols, count, bits, features, cotangent, degrees, weight, n_row, n_z):
    n, width = features.shape
    n_col = 2 * n_z
    n_plane = 2 * n_row
    slots = bits.shape[0]
    block = lambda k: pltpu.VMEM((k, n, width), BF16)
    sems = lambda k: pltpu.SemaphoreType.DMA((k,))
    slab = lambda k: pltpu.VMEM((k, width // n_plane, width), BF16)
    tile = jax.ShapeDtypeStruct((n, width), BF16)
    return pl.pallas_call(
        functools.partial(layer_kernel, n_row, n_z),
        out_shape=(tile, jax.ShapeDtypeStruct((width, width), F32), tile),
        in_specs=[pl.BlockSpec(memory_space=VMEM)] + [pl.BlockSpec(memory_space=pltpu.HBM)] * 7,
        out_specs=(pl.BlockSpec(memory_space=VMEM),) * 3,
        scratch_shapes=[
            pltpu.VMEM((n * n_row, n * n_col), BF16),
            pltpu.VMEM((slots + 1, 8, 8, 128), jnp.int32),
            pltpu.VMEM((2, slots), jnp.int32),
            pltpu.SMEM((2, slots), jnp.int32),
            pltpu.VMEM((1, slots), jnp.int32),
            pltpu.VMEM((1, slots), jnp.int32),
            pltpu.VMEM((1, n), jnp.int32),
            pltpu.VMEM(bits.shape, jnp.int32),
            pltpu.VMEM((n, width), BF16),
            pltpu.VMEM((n, width), BF16),
            pltpu.VMEM((width, width), BF16),
            sems(7), pltpu.SemaphoreType.DMA,
            block(n_row), block(n_col), block(n_col), block(n_z), block(n_z), block(n_z), block(2),
            block(n_row), pltpu.VMEM((n * n_row, width), F32), block(n_row), slab(n_plane), slab(n_plane), slab(n_z), slab(n_plane),
            sems(n_row), sems(n_row), sems(n_z), sems(n_col), sems(n_z), sems(n_z), sems(n_z),
            sems(n_z), sems(2), sems(n_z), sems(n_row), sems(n_row),
            sems(n_plane), sems(n_plane), sems(n_z), sems(n_z), sems(n_plane), sems(n_plane),
        ],
        compiler_params=pltpu.CompilerParams(
            collective_id=0, has_side_effects=True, vmem_limit_bytes=64 * 2**20
        ),
        name="layer",
    )(count, rows, cols, degrees, bits, features, cotangent, weight)


def swap_order(x, a, b):
    return x.reshape(-1, a, b, x.shape[-1]).swapaxes(1, 2).reshape(x.shape)


def per_device(features, cotangent, degrees, weight, tile_rows, tile_cols, tile_bits, tile_count):
    nodes, width = features.shape
    trows = nodes * lax.axis_size("col") // 128
    tcols = nodes * lax.axis_size("row") // 128
    n_row, n_col = lax.axis_size("row"), lax.axis_size("col")
    slots = tile_bits.shape[2]
    if n_row == 4 and n_col == 8 and nodes == width and trows * tcols < slots:
        results = layer(
            tile_rows[0], tile_cols[0], tile_count, tile_bits[0, 0],
            features, cotangent, degrees.reshape(1, nodes), weight, n_row, n_col // 2,
        )
        return place(results)
    at = build_adjacency(
        tile_count[0], tile_rows[0, 0], tile_cols[0, 0], tile_bits[0, 0], trows, tcols
    )
    deg = degrees[:, None].astype(F32)
    scaled = (cotangent.astype(F32) / deg).astype(BF16)
    feats = lax.all_gather(swap_order(features, 16, 8), "row", axis=0, tiled=True)
    grads = lax.all_gather(scaled, "col", axis=0, tiled=True)
    fwd = lax.dot_general(at, feats, (((0,), (0,)), ((), ())), preferred_element_type=F32)
    fwd = fwd.astype(BF16)
    local = lax.dot_general(fwd, grads, (((0,), (0,)), ((), ())), preferred_element_type=F32)
    weight_grad = lax.psum(local, ("row", "col"))
    summed = lax.psum_scatter(fwd, "col", scatter_dimension=0, tiled=True).astype(F32)
    aggregated = (summed / deg).astype(BF16)
    output = jnp.dot(aggregated, weight, preferred_element_type=F32).astype(BF16)
    bwd = jnp.dot(at, grads, preferred_element_type=F32).astype(BF16)
    back = swap_order(lax.psum_scatter(bwd, "row", scatter_dimension=0, tiled=True), 8, 16)
    input_grad = jnp.dot(back, weight.T, preferred_element_type=F32).astype(BF16)
    return output, weight_grad, input_grad


def solution(mesh):
    placed = (
        P(("col", "row"), None),
        P(("row", "col"), None),
        P(("row", "col")),
        P(),
        P("row", "col", None),
        P("row", "col", None),
        P("row", "col", None, None, None),
        P("row", "col"),
    )
    return jax.shard_map(
        per_device,
        mesh=mesh,
        in_specs=placed,
        out_specs=(P(("row", "col"), None), P(), P(("col", "row"), None)),
        check_vma=False,
    )
```

```python
import functools

import jax
import jax.numpy as jnp
from jax import lax
from jax.experimental import pallas as pl
from jax.experimental.pallas import tpu as pltpu
from jax.sharding import PartitionSpec as P

SMEM = pltpu.SMEM
VMEM = pltpu.VMEM
BF16 = jnp.bfloat16
F32 = jnp.float32


def build_kernel(trows, chunk, count_ref, rows_ref, cols_ref, bits_ref, out_ref, acc0, acc1):
    base = pl.program_id(0) * chunk
    zero = jnp.zeros(acc0.shape[1:], jnp.int32)

    def clear(p, carry):
        acc0[p] = zero
        acc1[p] = zero
        return carry

    lax.fori_loop(0, chunk * trows, clear, 0, unroll=4)
    count = count_ref[0]

    def add_pair(k, carry):
        for half, acc in enumerate((acc0, acc1)):
            s = 2 * k + half
            col = cols_ref[s] - base
            ok = (s < count) & (col >= 0) & (col < chunk)
            p = jnp.where(ok, col * trows + rows_ref[s], 0)
            words = bits_ref[s]
            word = (words[:8] | (words[8:] << 16)) & (0 - ok.astype(jnp.int32))
            for b in range(8):
                acc[p, b] += (word >> b) & 0x10001
        return carry

    lax.fori_loop(0, (count + 1) // 2, add_pair, 0)

    def convert(row, carry):
        lanes = pl.ds(pl.multiple_of(row * 128, 128), 128)
        for col in range(chunk):
            p = col * trows + row
            for b in range(8):
                v = acc0[p, b] + acc1[p, b]
                both = jnp.concatenate([v & 0xFFFF, v >> 16], axis=0)
                out_ref[pl.ds(col * 128 + b * 16, 16), lanes] = both.astype(F32).astype(BF16)
        return carry

    lax.fori_loop(0, trows, convert, 0)


def build_adjacency(count, rows, cols, bits, trows, tcols):
    chunk = max(d for d in range(1, tcols + 1) if tcols % d == 0 and d * trows <= 128)
    scratch = pltpu.VMEM((chunk * trows, 8, 8, 128), jnp.int32)
    return pl.pallas_call(
        functools.partial(build_kernel, trows, chunk),
        grid=(tcols // chunk,),
        out_shape=jax.ShapeDtypeStruct((tcols * 128, trows * 128), BF16),
        in_specs=[
            pl.BlockSpec(memory_space=SMEM),
            pl.BlockSpec(memory_space=SMEM),
            pl.BlockSpec(memory_space=SMEM),
            pl.BlockSpec(memory_space=VMEM),
        ],
        out_specs=pl.BlockSpec((chunk * 128, trows * 128), lambda g: (g, 0)),
        scratch_shapes=[scratch, scratch],
        compiler_params=pltpu.CompilerParams(vmem_limit_bytes=40 * 2**20),
        name="build_adjacency",
    )(count, rows, cols, bits)


MESH = pl.DeviceIdType.MESH


def copy_to(src, dst, send_sem, recv_sem, device):
    return pltpu.make_async_remote_copy(
        src_ref=src,
        dst_ref=dst,
        send_sem=send_sem,
        recv_sem=recv_sem,
        device_id=device,
        device_id_type=MESH,
    )


def dot(a, b, dims=((1,), (0,))):
    return lax.dot_general(a, b, (dims, ((), ())), preferred_element_type=F32)


def layer_kernel(
    n_row, n_z,
    count_ref, rows_hbm, cols_hbm, deg_hbm, bits_hbm, feat_hbm, cot_hbm, weight_hbm,
    out_ref, wgrad_ref, igrad_ref,
    at_ref, prefix, plan, plan_smem, rows_ref, cols_ref, deg_ref, bits_ref, feat_ref, cot_ref, weight_ref, load_s, plan_s,
    feats, grads, part, pair, sums, passed, arrived, back, back_sum, back_in, w_part, w_in, w_mid, w_all,
    feat_s, feat_r, grad_s, grad_r, relay_s, pair_s, pair_r, sum_s, sum_r, pass_r, back_s, back_r,
    w1_s, w1_r, w2_s, w2_r, w3_s, w3_r,
):
    n = feat_ref.shape[0]
    n_col = 2 * n_z
    n_plane = n_row * 2
    r = lax.axis_index("row")
    c = lax.axis_index("col")
    z = c // 2
    core = c % 2
    sibling = (r, z * 2 + 1 - core)

    me = r * 2 + core

    def plane_peer(i):
        q = (me + i) % n_plane
        return q, (q // 2, z * 2 + q % 2)

    def z_peer(i):
        zz = (z + i) % n_z
        return zz, (r, zz * 2 + core)

    def flip(i):
        return ((z // 2 + i // 2) % 2) * 2 + (z + i) % 2

    mate = flip(1)
    inner = z % 2 != z // 2
    end = z % 2 == z // 2

    def at_z(zz):
        return (r, zz * 2 + core)

    barrier = pltpu.get_barrier_semaphore()
    for i in range(1, n_plane):
        pl.semaphore_signal(barrier, inc=1, device_id=plane_peer(i)[1], device_id_type=MESH)
    for i in range(1, n_z):
        pl.semaphore_signal(barrier, inc=1, device_id=z_peer(i)[1], device_id_type=MESH)
    loads = [
        pltpu.make_async_copy(src, dst, load_s.at[k])
        for k, (src, dst) in enumerate(
            (
                (rows_hbm, rows_ref), (cols_hbm, cols_ref), (deg_hbm, deg_ref), (cot_hbm, cot_ref),
                (feat_hbm, feat_ref), (bits_hbm, bits_ref), (weight_hbm, weight_ref),
            )
        )
    ]
    for load in loads:
        load.start()

    i0 = lax.broadcasted_iota(jnp.int32, (n, n), 0)
    i1 = lax.broadcasted_iota(jnp.int32, (n, n), 1)
    placed = (i1 // 128) * 128 + (i1 % 16) * 8 + (i1 % 128) // 16
    order = (i0 == placed).astype(F32).astype(BF16)
    loads[2].wait()
    deg_row = deg_ref[...].astype(F32)
    deg_col = jnp.sum(jnp.where(i0 == i1, deg_row, 0.0), axis=1, keepdims=True)
    loads[3].wait()
    grads[c] = (cot_ref[...].astype(F32) / deg_col).astype(BF16)

    loads[4].wait()
    feats[r] = dot(feat_ref[...], order, ((0,), (0,))).astype(BF16)
    pl.semaphore_wait(barrier, n_plane + n_z - 2)

    def feat_copy(i):
        q = (r + i) % n_row
        return q, copy_to(feats.at[r], feats.at[r], feat_s.at[q], feat_r.at[r], (q, c))

    def grad_copy(i):
        return copy_to(grads.at[c], grads.at[c], grad_s.at[i], grad_r.at[c], at_z(flip(i)))

    def relay_copy(q):
        return copy_to(grads.at[q], grads.at[q], relay_s.at[q // 2], grad_r.at[q], sibling)

    for i in range(1, n_row):
        feat_copy(i)[1].start()
    for i in (3, 2, 1):
        grad_copy(i).start()
    relay_copy(c).start()

    loads[0].wait()
    loads[1].wait()
    trows = n * n_col // 128
    tcols = n * n_row // 128
    places = trows * tcols
    slots = rows_ref.shape[1]
    s0 = lax.broadcasted_iota(jnp.int32, (slots, slots), 0)
    s1 = lax.broadcasted_iota(jnp.int32, (slots, slots), 1)
    lane = lax.broadcasted_iota(jnp.int32, (1, slots), 1)
    place = jnp.where(lane < count_ref[...], cols_ref[...] * trows + rows_ref[...], places)
    key_row = (place * slots + lane).astype(F32)
    key_col = jnp.sum(jnp.where(s0 == s1, key_row, 0.0), axis=1, keepdims=True)
    rank = jnp.sum((key_row < key_col).astype(F32), axis=1, keepdims=True)
    picked = jnp.where(rank == s1.astype(F32), s0, 0)
    before = (key_col < (s1 * slots).astype(F32)).astype(jnp.int32)
    plan[0:1, :] = jnp.clip(jnp.sum(picked, axis=0, keepdims=True), 0, slots - 1)
    plan[1:2, :] = jnp.clip(jnp.sum(before, axis=0, keepdims=True), 0, slots)
    plan_copy = pltpu.make_async_copy(plan, plan_smem, plan_s)
    plan_copy.start()


    def arrive(ref, sem, slot):
        copy_to(ref.at[slot], ref.at[slot], sem.at[slot], sem.at[slot], sibling).wait_recv()

    plan_copy.wait()
    loads[5].wait()
    zero = jnp.zeros((8, 128), jnp.int32)
    for b in range(8):
        prefix[0, b] = zero

    def add_slot(k, totals):
        words = bits_ref[plan_smem[0, k]]
        word = words[:8] | (words[8:] << 16)
        totals = tuple(t + ((word >> b) & 0x10001) for b, t in enumerate(totals))
        for b in range(8):
            prefix[k + 1, b] = totals[b]
        return totals

    lax.fori_loop(0, slots, add_slot, (zero,) * 8, unroll=4)

    def place_row(row, carry):
        lanes = pl.ds(pl.multiple_of(row * 128, 128), 128)
        for col in range(tcols):
            p = col * trows + row
            first = plan_smem[1, p]
            last = plan_smem[1, p + 1]
            for b in range(8):
                v = prefix[last, b] - prefix[first, b]
                both = jnp.concatenate([v & 0xFFFF, v >> 16], axis=0)
                at_ref[pl.ds(col * 128 + b * 16, 16), lanes] = both.astype(F32).astype(BF16)
        return carry

    lax.fori_loop(0, trows, place_row, 0)

    for i in range(1, n_row):
        arrive(feats, feat_r, (r + i) % n_row)

    def forward(q):
        lanes = pl.ds(pl.multiple_of(q * n, n), n)
        total = dot(feats[0], at_ref[pl.ds(0, n), lanes])
        for k in range(1, n_row):
            total += dot(feats[k], at_ref[pl.ds(k * n, n), lanes])
        part[q] = total.astype(BF16)

    def pair_copy(zz):
        q = zz * 2 + 1 - core
        return copy_to(part.at[q], pair.at[zz], pair_s.at[zz], pair_r.at[zz], sibling)

    @pl.loop(0, n_z)
    def _(i):
        zz = flip(3 - i)
        forward(zz * 2 + 1 - core)
        pair_copy(zz).start()

    @pl.loop(0, n_z)
    def _(i):
        forward(flip(3 - i) * 2 + core)

    def paired(zz):
        arrive(pair, pair_r, zz)
        return part[zz * 2 + core].astype(F32) + pair[zz].astype(F32)

    def pass_copy(i):
        zz = flip(i)
        return copy_to(sums.at[zz], passed.at[zz], sum_s.at[zz], pass_r.at[zz], at_z(mate))

    def sum_copy(i):
        zz = flip(i)
        k = 0 if i == 1 else 1
        return copy_to(sums.at[zz], arrived.at[k], sum_s.at[zz], sum_r.at[k], at_z(zz))

    @pl.when(end)
    def _():
        sums[flip(3)] = paired(flip(3)).astype(BF16)
        pass_copy(3).start()
        sums[flip(2)] = paired(flip(2)).astype(BF16)
        pass_copy(2).start()

    sums[mate] = paired(mate).astype(BF16)
    sum_copy(1).start()

    def add_back(q):
        lanes = pl.ds(pl.multiple_of(q * n, n), n)
        return dot(at_ref[:, lanes], grads[q])

    back_sum[...] = add_back(c)

    for i in (1, 2, 3):
        q = flip(i) * 2 + core
        arrive(grads, grad_r, q)
        relay_copy(q).start()
        back_sum[...] += add_back(q)

    for i in range(n_z):
        q = flip(i) * 2 + 1 - core
        arrive(grads, grad_r, q)
        back_sum[...] += add_back(q)

    def back_copy(q):
        return copy_to(back.at[q], back_in.at[r], back_s.at[q], back_r.at[r], (q, c))

    for i in range(1, n_row):
        q = (r + i) % n_row
        back[q] = back_sum[pl.ds(pl.multiple_of(q * n, n), n), :].astype(BF16)
        back_copy(q).start()

    def add_passed(i):
        zz = flip(i)
        total = paired(zz)
        arrive(passed, pass_r, zz)
        sums[zz] = (total + passed[zz].astype(F32)).astype(BF16)
        sum_copy(i).start()

    local = dot(part[0], grads[0])
    for q in range(1, n_col):
        local += dot(part[q], grads[q])
    rounded = local.astype(BF16)
    slab = rounded.shape[0] // n_plane
    for d in range(n_plane):
        w_part[d] = rounded[d * slab : (d + 1) * slab]

    def w1_copy(i):
        q, device = plane_peer(i)
        return copy_to(w_part.at[q], w_in.at[me], w1_s.at[q], w1_r.at[me], device)

    def w2_copy(i):
        q, device = z_peer(i)
        return copy_to(w_mid.at[z], w_mid.at[z], w2_s.at[q], w2_r.at[z], device)

    def w3_copy(i):
        q, device = plane_peer(i)
        return copy_to(w_all.at[me], w_all.at[me], w3_s.at[q], w3_r.at[me], device)

    for i in range(1, n_plane):
        w1_copy(i).start()

    @pl.when(inner)
    def _():
        add_passed(2)

    w_in[me] = w_part[me]
    for i in range(1, n_plane):
        arrive(w_in, w1_r, (me + i) % n_plane)
    w_mid[z] = jnp.sum(w_in[...].astype(F32), axis=0).astype(BF16)
    for i in range(1, n_z):
        w2_copy(i).start()

    @pl.when(inner)
    def _():
        add_passed(3)

    for i in range(1, n_z):
        arrive(w_mid, w2_r, (z + i) % n_z)
    w_all[me] = jnp.sum(w_mid[...].astype(F32), axis=0).astype(BF16)
    for i in range(1, n_plane):
        w3_copy(i).start()

    loads[6].wait()
    total = back_sum[pl.ds(pl.multiple_of(r * n, n), n), :]
    for i in range(1, n_row):
        q = (r + i) % n_row
        arrive(back_in, back_r, q)
        total += back_in[q].astype(F32)
    ordered = dot(order, total.astype(BF16)).astype(BF16)
    igrad_ref[...] = dot(ordered, weight_ref[...], ((1,), (1,))).astype(BF16)

    total = paired(z)
    for k in range(2):
        arrive(arrived, sum_r, k)
        total += arrived[k].astype(F32)
    out_ref[...] = dot((total / deg_row).astype(BF16), weight_ref[...], ((0,), (0,))).astype(BF16)

    for i in range(1, n_plane):
        arrive(w_all, w3_r, (me + i) % n_plane)
    for d in range(n_plane):
        wgrad_ref[d * slab : (d + 1) * slab, :] = w_all[d].astype(F32)

    for i in range(1, n_row):
        feat_copy(i)[1].wait_send()
        back_copy((r + i) % n_row).wait_send()
    for i in (1, 2, 3):
        grad_copy(i).wait_send()
    sum_copy(1).wait_send()

    @pl.when(inner)
    def _():
        for i in (2, 3):
            sum_copy(i).wait_send()

    for i in range(n_z):
        zz = (z + i) % n_z
        relay_copy(zz * 2 + core).wait_send()
        pair_copy(zz).wait_send()

    for i in range(1, n_plane):
        w1_copy(i).wait_send()
        w3_copy(i).wait_send()

    @pl.when(end)
    def _():
        for i in (2, 3):
            pass_copy(i).wait_send()

    for i in range(1, n_z):
        w2_copy(i).wait_send()


def place_kernel(*refs):
    n = len(refs) // 2
    for k in range(n):
        refs[n + k][...] = refs[k][...]


def place(arrays):
    return pl.pallas_call(
        place_kernel,
        out_shape=tuple(jax.ShapeDtypeStruct(x.shape, x.dtype) for x in arrays),
        in_specs=[pl.BlockSpec(memory_space=VMEM)] * len(arrays),
        out_specs=(pl.BlockSpec(memory_space=VMEM),) * len(arrays),
        compiler_params=pltpu.CompilerParams(vmem_limit_bytes=64 * 2**20),
        name="place",
    )(*arrays)


def layer(rows, cols, count, bits, features, cotangent, degrees, weight, n_row, n_z):
    n, width = features.shape
    n_col = 2 * n_z
    n_plane = 2 * n_row
    slots = bits.shape[0]
    block = lambda k: pltpu.VMEM((k, n, width), BF16)
    sems = lambda k: pltpu.SemaphoreType.DMA((k,))
    slab = lambda k: pltpu.VMEM((k, width // n_plane, width), BF16)
    tile = jax.ShapeDtypeStruct((n, width), BF16)
    return pl.pallas_call(
        functools.partial(layer_kernel, n_row, n_z),
        out_shape=(tile, jax.ShapeDtypeStruct((width, width), F32), tile),
        in_specs=[pl.BlockSpec(memory_space=VMEM)] + [pl.BlockSpec(memory_space=pltpu.HBM)] * 7,
        out_specs=(pl.BlockSpec(memory_space=VMEM),) * 3,
        scratch_shapes=[
            pltpu.VMEM((n * n_row, n * n_col), BF16),
            pltpu.VMEM((slots + 1, 8, 8, 128), jnp.int32),
            pltpu.VMEM((2, slots), jnp.int32),
            pltpu.SMEM((2, slots), jnp.int32),
            pltpu.VMEM((1, slots), jnp.int32),
            pltpu.VMEM((1, slots), jnp.int32),
            pltpu.VMEM((1, n), jnp.int32),
            pltpu.VMEM(bits.shape, jnp.int32),
            pltpu.VMEM((n, width), BF16),
            pltpu.VMEM((n, width), BF16),
            pltpu.VMEM((width, width), BF16),
            sems(7), pltpu.SemaphoreType.DMA,
            block(n_row), block(n_col), block(n_col), block(n_z), block(n_z), block(n_z), block(2),
            block(n_row), pltpu.VMEM((n * n_row, width), F32), block(n_row), slab(n_plane), slab(n_plane), slab(n_z), slab(n_plane),
            sems(n_row), sems(n_row), sems(n_z), sems(n_col), sems(n_z), sems(n_z), sems(n_z),
            sems(n_z), sems(2), sems(n_z), sems(n_row), sems(n_row),
            sems(n_plane), sems(n_plane), sems(n_z), sems(n_z), sems(n_plane), sems(n_plane),
        ],
        compiler_params=pltpu.CompilerParams(
            collective_id=0, has_side_effects=True, vmem_limit_bytes=64 * 2**20
        ),
        name="layer",
    )(count, rows, cols, degrees, bits, features, cotangent, weight)


def swap_order(x, a, b):
    return x.reshape(-1, a, b, x.shape[-1]).swapaxes(1, 2).reshape(x.shape)


def per_device(features, cotangent, degrees, weight, tile_rows, tile_cols, tile_bits, tile_count):
    nodes, width = features.shape
    trows = nodes * lax.axis_size("col") // 128
    tcols = nodes * lax.axis_size("row") // 128
    n_row, n_col = lax.axis_size("row"), lax.axis_size("col")
    slots = tile_bits.shape[2]
    if n_row == 4 and n_col == 8 and nodes == width and trows * tcols < slots:
        results = layer(
            tile_rows[0], tile_cols[0], tile_count, tile_bits[0, 0],
            features, cotangent, degrees.reshape(1, nodes), weight, n_row, n_col // 2,
        )
        return place(results)
    at = build_adjacency(
        tile_count[0], tile_rows[0, 0], tile_cols[0, 0], tile_bits[0, 0], trows, tcols
    )
    deg = degrees[:, None].astype(F32)
    scaled = (cotangent.astype(F32) / deg).astype(BF16)
    feats = lax.all_gather(swap_order(features, 16, 8), "row", axis=0, tiled=True)
    grads = lax.all_gather(scaled, "col", axis=0, tiled=True)
    fwd = lax.dot_general(at, feats, (((0,), (0,)), ((), ())), preferred_element_type=F32)
    fwd = fwd.astype(BF16)
    local = lax.dot_general(fwd, grads, (((0,), (0,)), ((), ())), preferred_element_type=F32)
    weight_grad = lax.psum(local, ("row", "col"))
    summed = lax.psum_scatter(fwd, "col", scatter_dimension=0, tiled=True).astype(F32)
    aggregated = (summed / deg).astype(BF16)
    output = jnp.dot(aggregated, weight, preferred_element_type=F32).astype(BF16)
    bwd = jnp.dot(at, grads, preferred_element_type=F32).astype(BF16)
    back = swap_order(lax.psum_scatter(bwd, "row", scatter_dimension=0, tiled=True), 8, 16)
    input_grad = jnp.dot(back, weight.T, preferred_element_type=F32).astype(BF16)
    return output, weight_grad, input_grad


def solution(mesh):
    placed = (
        P(("col", "row"), None),
        P(("row", "col"), None),
        P(("row", "col")),
        P(),
        P("row", "col", None),
        P("row", "col", None),
        P("row", "col", None, None, None),
        P("row", "col"),
    )
    return jax.shard_map(
        per_device,
        mesh=mesh,
        in_specs=placed,
        out_specs=(P(("row", "col"), None), P(), P(("col", "row"), None)),
        check_vma=False,
    )
```
